512 devices in a mesh: seq: 8 (over x, core), owner: 64 (over y, z).
Axes of the slice: x: 4, y: 4, z: 16, core: 2. Of those that a mesh axis runs over, the one named last changes fastest.
Arguments:
- queries: bfloat16 [64, 512, 2048], P('owner', 'seq'), may hold values from -16 to 16
- keys: bfloat16 [64, 512, 2048], P('owner', 'seq'), may hold values from -16 to 16
- values: bfloat16 [64, 512, 2048], P('owner', 'seq'), may hold values from -6 to 6
- text_grad: bfloat16 [64, 512, 2048], P('owner', 'seq'), may hold values from -6 to 6
- active: int32 [64, 512], P('owner', 'seq'), may hold values from 0 to 1, as said below
- target: int32 [64, 512], P('owner', 'seq'), may hold values from 0 to 63, as said below
- codes: bfloat16 [64, 472, 8, 1024], P('owner', 'seq'), may hold values from -12 to 12
- depth_cot: bfloat16 [64, 472, 8, 1024], P('owner', 'seq'), may hold values from -6 to 6
- w_in: bfloat16 [2097152], P(('seq', 'owner')), may hold values from -0.125 to 0.125
- norm_gain: bfloat16 [1024], replicated, may hold values from 0.25 to 1.75
- w_qkv: bfloat16 [1572864], P(('seq', 'owner')), may hold values from -4 to 4
- w_out: bfloat16 [524288], P(('seq', 'owner')), may hold values from -0.25 to 0.25
Outputs:
- query_grad: bfloat16 [64, 512, 2048], P('owner', 'seq')
- key_grad: bfloat16 [64, 512, 2048], P('owner', 'seq')
- value_grad: bfloat16 [64, 512, 2048], P('owner', 'seq')
The draws below stay inside these ranges and needn't reach their ends.
Inputs may be any that keep to these rules, and one draw needn't show every extreme that they name: In every block of 64 positions of a sequence exactly 59 frames are active. For each block of positions, every owner index is the target of exactly 59 active frames; one sequence's block sends at most 2 active frames to one owner, and exactly 2 to some owner. Targets of inactive frames are arbitrary.
All inputs are finite; a program needn't handle non-finite values.
Results may differ from the reference program's by a relative error of at most 0.035.
Values may be sent and summed in bfloat16 or wider, within the bound.
No kernel may reach another device: no remote copies, remote signals or barrier semaphores. Data moves between devices by JAX's collectives and lax.ppermute only.
A program may use at most 128 MiB of HBM per device.

```python
import jax
import jax.numpy as jnp
import numpy as np
from jax import lax

HEADS = 16
HEAD = 128
D_DEP = 1024
DHEADS = 8
DHEAD = 64
CODES = 8
FRAMES_DEV = 64
D_CTX = 2048
BATCH = 64
LENGTH = 512
ACT = 59
CAP = 2
RECV = 472
N_SEQ = 8


def routing_tables(key):
    row_keys = jax.random.split(key, N_SEQ)
    distinct = (ACT + CAP - 1) // CAP
    choose = np.arange(ACT) % distinct
    fixed_offsets = jnp.array([1, BATCH - 1, BATCH // 2], jnp.int32)
    fixed_scores = jnp.array([-3, -2, -1], jnp.int32)

    def one_row(row_key):
        order_key, frame_key, spare_key = jax.random.split(row_key, 3)
        scores = jax.random.permutation(order_key, BATCH).astype(jnp.int32)
        scores = scores.at[fixed_offsets].set(fixed_scores)
        offsets = jnp.argsort(scores, stable=True)[:distinct][choose].astype(jnp.int32)
        frame_keys = jax.random.split(frame_key, BATCH)
        shuffled = jax.vmap(lambda single_key: jax.random.permutation(single_key, FRAMES_DEV))(frame_keys)
        sources = jnp.arange(BATCH, dtype=jnp.int32)[:, None]
        aimed = (sources + offsets[None, :]) % BATCH
        filler = jax.random.randint(spare_key, (BATCH, FRAMES_DEV), 0, BATCH)
        chosen = shuffled[:, :ACT]
        row_index = jnp.broadcast_to(sources, (BATCH, ACT))
        target_row = filler.at[row_index, chosen].set(aimed.astype(jnp.int32))
        active_row = jnp.zeros((BATCH, FRAMES_DEV), jnp.int32).at[row_index, chosen].set(1)
        return (active_row, target_row)
    active_all, target_all = jax.vmap(one_row)(row_keys)
    active_all = jnp.transpose(active_all, (1, 0, 2)).reshape(BATCH, N_SEQ * FRAMES_DEV)
    target_all = jnp.transpose(target_all, (1, 0, 2)).reshape(BATCH, N_SEQ * FRAMES_DEV)
    return (active_all.astype(jnp.int32), target_all.astype(jnp.int32))


def draw_active(key, part):
    active_all, target_all = routing_tables(key)
    return active_all


def draw_target(key, part):
    active_all, target_all = routing_tables(key)
    return target_all


def draw_queries(key, part):
    key = jax.random.fold_in(key, 11)
    drawn = jax.random.normal(key, (BATCH, LENGTH, D_CTX), jnp.float32)
    return jnp.clip(drawn, -16.0, 16.0).astype(jnp.bfloat16)


def draw_keys(key, part):
    key = jax.random.fold_in(key, 23)
    drawn = jax.random.normal(key, (BATCH, LENGTH, D_CTX), jnp.float32)
    return jnp.clip(drawn, -16.0, 16.0).astype(jnp.bfloat16)


def draw_codes(key, part):
    key = jax.random.fold_in(key, 37)
    first_key = jax.random.fold_in(key, 0)
    drawn = jnp.clip(0.2 * jax.random.normal(first_key, (BATCH, RECV, CODES, D_DEP), jnp.float32), -1.2, 1.2)
    return jnp.clip(drawn, -12.0, 12.0).astype(jnp.bfloat16)


def draw_w_qkv(key, part):
    key = jax.random.fold_in(key, 41)
    first_key = jax.random.fold_in(key, 0)
    drawn = jax.random.normal(first_key, (D_DEP, 3, DHEADS, DHEAD), jnp.float32) * D_DEP ** (-0.5)
    return jnp.clip(drawn, -4.0, 4.0).reshape(-1).astype(jnp.bfloat16)


def level_of(key, extent, cuts, smallest, high):
    loudness, own = 1.0, jax.random.fold_in(key, 6)
    for position, parts in cuts:
        heights = jnp.exp(jax.random.uniform(jax.random.fold_in(own, position), (parts,), jnp.float32, smallest / len(cuts), high / len(cuts)))
        loudness = loudness * jnp.repeat(heights, extent[position] // parts).reshape([-1 if axis == position else 1 for axis in range(len(extent))])
    return loudness


def scatter_about(stream_key, extent, scale, reach, shards=(), kind=jnp.bfloat16):
    values = jax.random.normal(stream_key, extent, jnp.float32) * scale
    if len(shards) > 0:
        values = level_of(stream_key, extent, shards, -0.22, 0.18) * values
    return jnp.clip(values, min=-reach, max=reach).astype(kind)


def setup_inputs(seed: int = 0) -> dict:
    key_list = jax.random.split(jax.random.key(seed), 13)
    queries = draw_queries(jax.random.fold_in(key_list[12], 71), 0)
    keys = draw_keys(jax.random.fold_in(key_list[12], 71), 0)
    values = scatter_about(key_list[2], (BATCH, LENGTH, D_CTX), 1.0, 6.0, ((0, 64), (1, 8)))
    text_grad = scatter_about(key_list[3], (BATCH, LENGTH, D_CTX), 1.0, 6.0, ((0, 64), (1, 8)))
    active = draw_active(jax.random.fold_in(key_list[12], 71), 0)
    target = draw_target(jax.random.fold_in(key_list[12], 71), 0)
    codes = draw_codes(jax.random.fold_in(key_list[12], 71), 0)
    depth_cot = scatter_about(key_list[7], (BATCH, RECV, CODES, D_DEP), 1.0, 6.0, ((0, 64), (1, 8)))
    w_in = scatter_about(key_list[8], (D_CTX * D_DEP,), D_CTX ** -0.5, 0.125, ((0, 512),))
    norm_gain = jnp.clip(1.0 + 0.15 * jax.random.normal(key_list[9], (D_DEP,), jnp.float32), 0.25, 1.75).astype(jnp.bfloat16)
    w_qkv = draw_w_qkv(jax.random.fold_in(key_list[12], 71), 0)
    w_out = scatter_about(key_list[11], (DHEADS * DHEAD * D_DEP,), (DHEADS * DHEAD) ** -0.5, 0.25, ((0, 512),))
    return dict(queries=queries, keys=keys, values=values, text_grad=text_grad, active=active, target=target, codes=codes, depth_cot=depth_cot, w_in=w_in, norm_gain=norm_gain, w_qkv=w_qkv, w_out=w_out)


def attend(query_rows, key_rows, value_rows, offset):
    query_count = query_rows.shape[0]
    key_count = key_rows.shape[0]
    query_heads = query_rows.astype(jnp.float32).reshape(query_count, HEADS, HEAD)
    key_heads = key_rows.astype(jnp.float32).reshape(key_count, HEADS, HEAD)
    value_heads = value_rows.astype(jnp.float32).reshape(key_count, HEADS, HEAD)
    scores = jnp.einsum('qhd,khd->hqk', query_heads, key_heads) * HEAD ** (-0.5)
    query_pos = offset + jnp.arange(query_count, dtype=jnp.int32)
    key_pos = jnp.arange(key_count, dtype=jnp.int32)
    allowed = key_pos[None, None, :] <= query_pos[None, :, None]
    scores = jnp.where(allowed, scores, -1e+30)
    weights = jax.nn.softmax(scores, axis=-1).astype(jnp.bfloat16)
    mixed = jnp.einsum('hqk,khd->qhd', weights.astype(jnp.float32), value_heads)
    return mixed.reshape(query_count, HEADS * HEAD)

def depth_layer(frame_rows, code_rows, w_in, norm_gain, w_qkv, w_out):
    hidden = jnp.dot(frame_rows.astype(jnp.float32), w_in.astype(jnp.float32))[:, None, :] + code_rows.astype(jnp.float32)
    scale = lax.rsqrt(lax.optimization_barrier(jnp.mean(hidden * hidden, axis=-1, keepdims=True)) + 1e-05)
    normed = (hidden * scale * norm_gain.astype(jnp.float32)).astype(jnp.bfloat16)
    row_count = hidden.shape[0]
    flat = normed.reshape(row_count * CODES, D_DEP)
    projected = jnp.dot(flat.astype(jnp.float32), w_qkv.astype(jnp.float32)).astype(jnp.bfloat16)
    projected = projected.reshape(row_count, CODES, 3, DHEADS, DHEAD).astype(jnp.float32)
    dquery = projected[:, :, 0]
    dkey = projected[:, :, 1]
    dvalue = projected[:, :, 2]
    scores = jnp.einsum('rchd,rkhd->rhck', dquery, dkey) * DHEAD ** (-0.5)
    causal = jnp.arange(CODES)[None, :] <= jnp.arange(CODES)[:, None]
    scores = jnp.where(causal[None, None], scores, -1e+30)
    weights = jax.nn.softmax(scores, axis=-1).astype(jnp.bfloat16)
    mixed = jnp.einsum('rhck,rkhd->rchd', weights.astype(jnp.float32), dvalue).astype(jnp.bfloat16)
    mixed = mixed.reshape(row_count * CODES, DHEADS * DHEAD)
    update = jnp.dot(mixed.astype(jnp.float32), w_out.astype(jnp.float32))
    return hidden + update.reshape(hidden.shape)

def depth_grad(frame_rows, code_rows, cot_rows, w_in, norm_gain, w_qkv, w_out):

    def forward(rows_in):
        return depth_layer(rows_in, code_rows, w_in, norm_gain, w_qkv, w_out)
    unused, pull = jax.vjp(forward, frame_rows)
    return pull(cot_rows.astype(jnp.float32))[0]

def reference(queries, keys, values, text_grad, active, target, codes, depth_cot, w_in, norm_gain, w_qkv, w_out):
    frame_count = FRAMES_DEV
    matrix_in = w_in.reshape(D_CTX, D_DEP)
    matrix_qkv = w_qkv.reshape(D_DEP, 3 * DHEADS * DHEAD)
    matrix_out = w_out.reshape(DHEADS * DHEAD, D_DEP)
    blocks = jnp.arange(N_SEQ, dtype=jnp.int32)

    def forward_block(block):
        start = block * frame_count
        query_block = lax.dynamic_slice_in_dim(queries, start, frame_count, 1)

        def single(query_rows, key_rows, value_rows):
            return attend(query_rows, key_rows, value_rows, start)
        return jax.vmap(single)(query_block, keys, values).astype(jnp.bfloat16)
    context = lax.map(forward_block, blocks)
    owner_ids = jnp.arange(BATCH, dtype=jnp.int32)

    def depth_block(block):
        start = block * frame_count
        live = lax.dynamic_slice_in_dim(active, start, frame_count, 1).reshape(-1)
        aimed = lax.dynamic_slice_in_dim(target, start, frame_count, 1).reshape(-1)
        matches = jnp.where((aimed[:, None] == owner_ids[None, :]) & (live[:, None] == 1), 1, 0).astype(jnp.int32)
        ranking = lax.optimization_barrier(jnp.sum((jnp.cumsum(matches, axis=0) - matches) * matches, axis=1))
        place = jnp.where(live == 1, aimed, BATCH)
        source = jnp.zeros((BATCH, ACT), jnp.int32).at[place, ranking].set(jnp.arange(BATCH * frame_count, dtype=jnp.int32), mode='drop')
        flat_context = context[block].reshape(BATCH * frame_count, D_CTX)
        frame_rows = flat_context[source.reshape(-1)]
        code_block = lax.dynamic_slice_in_dim(codes, block * ACT, ACT, 1).reshape(BATCH * ACT, CODES, D_DEP)
        cot_block = lax.dynamic_slice_in_dim(depth_cot, block * ACT, ACT, 1).reshape(BATCH * ACT, CODES, D_DEP)
        row_grads = depth_grad(frame_rows, code_block, cot_block, matrix_in, norm_gain, matrix_qkv, matrix_out)
        back_rows = row_grads[aimed * ACT + ranking].astype(jnp.float32)
        carried = jnp.where(live[:, None] == 1, back_rows, jnp.float32(0.0))
        return carried.reshape(BATCH, frame_count, D_CTX)
    carried = lax.map(depth_block, blocks)
    carried = jnp.transpose(carried, (1, 0, 2, 3)).reshape(BATCH, LENGTH, D_CTX)
    out_grad = (text_grad.astype(jnp.float32) + carried).astype(jnp.bfloat16)

    def backward_block(totals, block):
        start = block * frame_count
        query_block = lax.dynamic_slice_in_dim(queries, start, frame_count, 1)
        grad_block = lax.dynamic_slice_in_dim(out_grad, start, frame_count, 1)

        def single(query_rows, key_rows, value_rows, grad_rows):

            def forward(first, second, third):
                return attend(first, second, third, start)
            unused, pull = jax.vjp(forward, query_rows, key_rows, value_rows)
            return pull(grad_rows.astype(jnp.float32))
        query_part, key_part, value_part = jax.vmap(single)(query_block, keys, values, grad_block)
        totals = (totals[0] + key_part.astype(jnp.float32), totals[1] + value_part.astype(jnp.float32))
        return (totals, query_part)
    zeros = jnp.zeros((BATCH, LENGTH, D_CTX), jnp.float32)
    totals, query_parts = lax.scan(backward_block, (zeros, zeros), blocks)
    query_grad = jnp.transpose(query_parts, (1, 0, 2, 3)).reshape(BATCH, LENGTH, D_CTX).astype(jnp.bfloat16)
    return (query_grad, totals[0].astype(jnp.bfloat16), totals[1].astype(jnp.bfloat16))
```

```python
import jax
import jax.numpy as jnp
from jax import lax
from jax.experimental import pallas as pl
from jax.experimental.pallas import tpu as pltpu
from jax.sharding import Mesh
from jax.sharding import PartitionSpec as P

HEADS = 16
HEAD = 128
D_DEP = 1024
DHEADS = 8
DHEAD = 64
CODES = 8
D_CTX = 2048
FRAMES = 64
SEQ = 8
OWNERS = 64
CAP = 2
SLOTS = OWNERS * CAP
RECEIVED = 59
LENGTH = SEQ * FRAMES
COLS = D_CTX // SEQ
ROWS = RECEIVED * CODES
PADDED = 512
CHUNK = 256
GROUP = 128
EMPTY = 2.0**100
BF = jnp.bfloat16
F32 = jnp.float32


def dot(a, b):
    return jnp.dot(a, b, preferred_element_type=F32)


def dot_nt(a, b):
    return lax.dot_general(a, b, (((1,), (1,)), ((), ())), preferred_element_type=F32)


def dot_tn(a, b):
    return lax.dot_general(a, b, (((0,), (0,)), ((), ())), preferred_element_type=F32)


def iota(shape, axis):
    return lax.broadcasted_iota(jnp.int32, shape, axis)


def call(kernel, out_shape, name, **options):
    limit = options.pop("vmem", 32)
    return pl.pallas_call(
        kernel,
        out_shape=out_shape,
        name=name,
        compiler_params=pltpu.CompilerParams(vmem_limit_bytes=limit * 2**20),
        **options,
    )


def weight_kernel(gathered_ref, out_ref):
    row = iota((512, 512), 0)
    col = iota((512, 512), 1)
    none = jnp.full((512, 512), -1, jnp.int32)

    def pick(first, second, third, fourth):
        source = jnp.where(
            row < 256, first, jnp.where(row < 384, second, jnp.where(row < 448, third, fourth))
        )
        return (col == source).astype(F32).astype(BF)

    in_row = ((row >> 2) << 3) + (row & 3)
    wide = row - 256
    wide_base = (wide >> 1) << 3
    wide_odd = (wide & 1) == 1
    tail = row - 384
    tail_base = (tail >> 1) << 3
    tail_odd = (tail & 1) == 1
    out_row = ((row - 448) << 3) + 7
    left_left = pick(
        in_row,
        jnp.where(wide_odd, none, wide_base + 4),
        jnp.where(tail_odd, none, tail_base + 5),
        out_row,
    )
    left_right = pick(
        none, jnp.where(wide_odd, wide_base + 5, none), jnp.where(tail_odd, tail_base + 6, none), none
    )
    right_left = pick(
        none,
        jnp.where(wide_odd, wide_base + 6, none),
        jnp.where(tail_odd, none, tail_base + 256 + 5),
        none,
    )
    right_right = pick(
        in_row,
        jnp.where(wide_odd, none, wide_base + 4),
        jnp.where(tail_odd, tail_base + 256 + 6, none),
        out_row,
    )
    left = gathered_ref[:, :512]
    right = gathered_ref[:, 512:]
    out_ref[:, :512] = (dot(left_left, left) + dot(left_right, right)).astype(BF)
    out_ref[:, 512:] = (dot(right_left, left) + dot(right_right, right)).astype(BF)


def pack_kernel(first_ref, second_ref, third_ref, out_ref):
    for part in range(SEQ):
        for place, ref in enumerate((first_ref, second_ref, third_ref)):
            out_ref[part, :, place * COLS : (place + 1) * COLS] = ref[
                :, part * COLS : (part + 1) * COLS
            ]


def unpack_kernel(packed_ref, first_ref, second_ref, third_ref):
    for part in range(SEQ):
        for place, ref in enumerate((first_ref, second_ref, third_ref)):
            ref[:, part * COLS : (part + 1) * COLS] = packed_ref[
                part, :, place * COLS : (place + 1) * COLS
            ]


def head_weights(packed_ref, head):
    base = head * HEAD
    query = packed_ref[:, base : base + HEAD]
    key = packed_ref[:, COLS + base : COLS + base + HEAD]
    value = packed_ref[:, 2 * COLS + base : 2 * COLS + base + HEAD]
    scores = dot_nt(query, key) * HEAD ** (-0.5)
    allowed = iota((LENGTH, LENGTH), 1) <= iota((LENGTH, LENGTH), 0)
    scores = jnp.where(allowed, scores, -1e30)
    raised = jnp.exp(scores - jnp.max(scores, axis=1, keepdims=True))
    weights = raised * (1.0 / jnp.sum(raised, axis=1, keepdims=True))
    return query, key, value, weights


def forward_kernel(packed_ref, w_in_ref, out_ref):
    total = None
    for head in range(2):
        unused_q, unused_k, value, weights = head_weights(packed_ref, head)
        context = dot(weights.astype(BF), value).astype(BF)
        part = dot(context, w_in_ref[head * HEAD : (head + 1) * HEAD, :])
        total = part if total is None else total + part
    out_ref[...] = total.astype(BF)


def backward_kernel(packed_ref, grad_ref, out_ref):
    for head in range(2):
        base = head * HEAD
        query, key, value, weights = head_weights(packed_ref, head)
        grad = grad_ref[:, base : base + HEAD]
        weight_grad = dot_nt(grad, value).astype(BF).astype(F32)
        inner = jnp.sum(weight_grad * weights, axis=1, keepdims=True)
        score_grad = (weights * (weight_grad - inner) * HEAD ** (-0.5)).astype(BF)
        out_ref[:, base : base + HEAD] = dot(score_grad, key).astype(BF)
        out_ref[:, COLS + base : COLS + base + HEAD] = dot_tn(score_grad, query).astype(BF)
        out_ref[:, 2 * COLS + base : 2 * COLS + base + HEAD] = dot_tn(
            weights.astype(BF), grad
        ).astype(BF)


def routing(target_ref, active_ref):
    down = iota((FRAMES, FRAMES), 0)
    across = iota((FRAMES, FRAMES), 1)
    target_row = target_ref[...].astype(F32)
    live_row = (active_ref[...] == 1).astype(F32)
    target_col = jnp.sum(jnp.where(down == across, target_row, 0.0), axis=1, keepdims=True)
    live_col = jnp.sum(jnp.where(down == across, live_row, 0.0), axis=1, keepdims=True)
    same = target_col == target_row
    earlier_row = jnp.sum(jnp.where(same & (down < across), live_col, 0.0), axis=0, keepdims=True)
    earlier_col = jnp.sum(jnp.where(same & (across < down), live_row, 0.0), axis=1, keepdims=True)
    return (target_row, live_row, earlier_row), (target_col, live_col, earlier_col)


def send_kernel(parts_ref, target_ref, active_ref, out_ref):
    rows = parts_ref[0].astype(F32)
    for part in range(1, SEQ):
        rows = rows + parts_ref[part].astype(F32)
    (target, live, earlier), unused = routing(target_ref, active_ref)
    slot = iota((SLOTS, FRAMES), 0)
    chosen = (
        (target == (slot >> 1).astype(F32)) & (live > 0.5) & (earlier == (slot & 1).astype(F32))
    ).astype(F32)
    sent = dot(chosen.astype(BF), rows.astype(BF))
    filled = jnp.sum(chosen, axis=1, keepdims=True) > 0.5
    out_ref[...] = jnp.where(filled, sent, EMPTY).astype(BF)


def return_kernel(returned_ref, target_ref, active_ref, text_ref, w_in_ref, out_ref, rows_ref):
    @pl.when(pl.program_id(0) == 0)
    def _():
        unused, (target, live, earlier) = routing(target_ref, active_ref)
        slot = iota((FRAMES, SLOTS), 1)
        chosen = (
            (target == (slot >> 1).astype(F32)) & (live > 0.5) & (earlier == (slot & 1).astype(F32))
        ).astype(F32)
        rows_ref[...] = dot(chosen.astype(BF), returned_ref[...]).astype(BF)

    carried = dot_nt(rows_ref[...], w_in_ref[0]).astype(BF).astype(F32)
    out_ref[0] = (text_ref[...].astype(F32) + carried).astype(BF)


def depth_kernel(
    slots_ref,
    codes_ref,
    cot_ref,
    gain_ref,
    weights_ref,
    out_ref,
    w_qkv,
    w_out,
    hidden_s,
    cot_s,
    grads_s,
    frames_s,
    sems,
):
    copies = []
    for part in range(SEQ):
        low = part * 128
        pairs = (
            (weights_ref.at[part, 256:384, :], w_qkv.at[low : low + 128, :1024]),
            (weights_ref.at[part, 384:448, :512], w_qkv.at[low : low + 64, 1024:]),
            (weights_ref.at[part, 384:448, 512:], w_qkv.at[low + 64 : low + 128, 1024:]),
            (weights_ref.at[part, 448:512, :], w_out.at[part * 64 : part * 64 + 64, :]),
        )
        for source, goal in pairs:
            copies.append(pltpu.make_async_copy(source, goal, sems.at[len(copies)]))
    for copy in copies:
        copy.start()

    slots = slots_ref[...]
    live_col = (slots[:, 0:1].astype(F32) < EMPTY * 0.5).astype(F32)
    down = iota((SLOTS, SLOTS), 0)
    across = iota((SLOTS, SLOTS), 1)
    live_row = jnp.sum(jnp.where(down == across, live_col, 0.0), axis=0, keepdims=True)
    rank_row = jnp.sum(jnp.where(down < across, live_col, 0.0), axis=0, keepdims=True)
    rank_col = jnp.sum(jnp.where(across < down, live_row, 0.0), axis=1, keepdims=True)

    spread = (
        (live_row > 0.5) & (rank_row == (iota((PADDED, SLOTS), 0) >> 3).astype(F32))
    ).astype(F32)
    spare = jnp.zeros((PADDED - ROWS, D_DEP), F32)
    hidden_s[...] = dot(spread.astype(BF), slots) + jnp.concatenate(
        [codes_ref[...].astype(F32), spare], axis=0
    )
    cot_s[...] = jnp.concatenate([cot_ref[...].astype(F32), spare], axis=0)
    gain = gain_ref[...].astype(F32)
    for copy in copies:
        copy.wait()

    row = iota((GROUP, GROUP), 0)
    col = iota((GROUP, GROUP), 1)
    allowed = ((row >> 3) == (col >> 3)) & (col <= row)
    first_half = iota((GROUP, GROUP), 1) < DHEAD
    nothing = jnp.zeros((GROUP, GROUP), BF)
    width = DHEADS * DHEAD
    for chunk in range(PADDED // CHUNK):
        low = chunk * CHUNK
        hidden = hidden_s[low : low + CHUNK, :]
        cot = cot_s[low : low + CHUNK, :]
        scale = lax.rsqrt(jnp.sum(hidden * hidden, axis=1, keepdims=True) * (1.0 / D_DEP) + 1e-05)
        normed = (hidden * scale * gain).astype(BF)
        projected = dot(normed, w_qkv[...]).astype(BF)
        mixed_grad = dot_nt(cot.astype(BF), w_out[...]).astype(BF)
        for group in range(CHUNK // GROUP):
            rows = slice(group * GROUP, (group + 1) * GROUP)
            for pair in range(DHEADS // 2):
                lanes = pair * 128
                query = projected[rows, lanes : lanes + 128]
                key = projected[rows, width + lanes : width + lanes + 128]
                value = projected[rows, 2 * width + lanes : 2 * width + lanes + 128]
                grad = mixed_grad[rows, lanes : lanes + 128]
                totals = [None, None, None]
                for half in range(2):
                    own = first_half if half == 0 else ~first_half
                    own_query = jnp.where(own, query, nothing)
                    own_key = jnp.where(own, key, nothing)
                    own_grad = jnp.where(own, grad, nothing)
                    scores = dot_nt(own_query, key) * DHEAD ** (-0.5)
                    scores = jnp.where(allowed, scores, -1e30)
                    raised = jnp.exp(scores - jnp.max(scores, axis=1, keepdims=True))
                    weights = raised * (1.0 / jnp.sum(raised, axis=1, keepdims=True))
                    weight_grad = dot_nt(own_grad, value).astype(BF).astype(F32)
                    inner = jnp.sum(weight_grad * weights, axis=1, keepdims=True)
                    score_grad = (weights * (weight_grad - inner) * DHEAD ** (-0.5)).astype(BF)
                    terms = (
                        dot(score_grad, own_key),
                        dot_tn(score_grad, own_query),
                        dot_tn(weights.astype(BF), own_grad),
                    )
                    totals = [t if s is None else s + t for s, t in zip(totals, terms)]
                for place, total in enumerate(totals):
                    start = place * width + lanes
                    grads_s[rows, start : start + 128] = total.astype(BF)
        normed_grad = dot_nt(grads_s[...], w_qkv[...]).astype(BF).astype(F32) * gain
        inner = jnp.sum(normed_grad * hidden, axis=1, keepdims=True) * (1.0 / D_DEP)
        hidden_grad = cot + scale * normed_grad - hidden * (scale * scale * scale * inner)
        frames = jnp.sum(hidden_grad.reshape(CHUNK // CODES, CODES, D_DEP), axis=1)
        frames_s[low // CODES : (low + CHUNK) // CODES, :] = frames

    back = ((live_col > 0.5) & (rank_col == iota((SLOTS, FRAMES), 1).astype(F32))).astype(F32)
    out_ref[...] = dot(back.astype(BF), frames_s[...].astype(BF)).astype(BF)


def exchange(array, axis):
    return lax.all_to_all(array, axis, split_axis=0, concat_axis=0, tiled=True)


def shards(
    queries,
    keys,
    values,
    text_grad,
    active,
    target,
    codes,
    depth_cot,
    w_in,
    norm_gain,
    w_qkv,
    w_out,
):
    owner = ("y", "z")
    mine = jnp.concatenate([w_in, w_qkv, w_out]).reshape(1, 8, D_DEP)
    along_z = exchange(jnp.broadcast_to(mine, (16, 8, D_DEP)), "z")
    along_y = exchange(jnp.broadcast_to(along_z.reshape(1, 128, D_DEP), (4, 128, D_DEP)), "y")
    own_weights = call(weight_kernel, jax.ShapeDtypeStruct((512, D_DEP), BF), "sort_weights")(
        along_y.reshape(512, D_DEP)
    )
    all_weights = lax.all_gather(own_weights, "seq", axis=0, tiled=True).reshape(SEQ, 512, D_DEP)

    packed = call(pack_kernel, jax.ShapeDtypeStruct((SEQ, FRAMES, 3 * COLS), BF), "pack_qkv")(
        queries[0], keys[0], values[0]
    )
    packed = exchange(packed, "seq").reshape(LENGTH, 3 * COLS)
    parts = call(
        forward_kernel,
        jax.ShapeDtypeStruct((LENGTH, D_DEP), BF),
        "attention_forward",
        grid=(1,),
        in_specs=[
            pl.BlockSpec((LENGTH, 3 * COLS), lambda i: (0, 0)),
            pl.BlockSpec((COLS, D_DEP), lambda i: (0, 0)),
        ],
        out_specs=pl.BlockSpec((LENGTH, D_DEP), lambda i: (0, 0)),
    )(packed, own_weights)
    parts = exchange(parts.reshape(SEQ, FRAMES, D_DEP), "seq")
    sent = call(send_kernel, jax.ShapeDtypeStruct((SLOTS, D_DEP), BF), "send_rows")(
        parts, target, active
    )
    slots = exchange(sent.reshape(OWNERS, CAP, D_DEP), owner).reshape(SLOTS, D_DEP)
    vmem = pl.BlockSpec(memory_space=pltpu.VMEM)
    grads = call(
        depth_kernel,
        jax.ShapeDtypeStruct((SLOTS, D_DEP), BF),
        "depth_layer",
        in_specs=[vmem, vmem, vmem, vmem, pl.BlockSpec(memory_space=pl.ANY)],
        out_specs=vmem,
        scratch_shapes=[
            pltpu.VMEM((D_DEP, 3 * DHEADS * DHEAD), BF),
            pltpu.VMEM((DHEADS * DHEAD, D_DEP), BF),
            pltpu.VMEM((PADDED, D_DEP), F32),
            pltpu.VMEM((PADDED, D_DEP), F32),
            pltpu.VMEM((CHUNK, 3 * DHEADS * DHEAD), BF),
            pltpu.VMEM((FRAMES, D_DEP), F32),
            pltpu.SemaphoreType.DMA((4 * SEQ,)),
        ],
        vmem=48,
    )(
        slots,
        codes.reshape(ROWS, D_DEP),
        depth_cot.reshape(ROWS, D_DEP),
        norm_gain.reshape(1, D_DEP),
        all_weights,
    )
    returned = exchange(grads.reshape(OWNERS, CAP, D_DEP), owner).reshape(SLOTS, D_DEP)
    out_grad = call(
        return_kernel,
        jax.ShapeDtypeStruct((SEQ, FRAMES, COLS), BF),
        "return_rows",
        grid=(SEQ,),
        in_specs=[
            pl.BlockSpec((SLOTS, D_DEP), lambda i: (0, 0)),
            pl.BlockSpec((1, FRAMES), lambda i: (0, 0)),
            pl.BlockSpec((1, FRAMES), lambda i: (0, 0)),
            pl.BlockSpec((FRAMES, COLS), lambda i: (0, i)),
            pl.BlockSpec((1, COLS, D_DEP), lambda i: (i, 0, 0)),
        ],
        out_specs=pl.BlockSpec((1, FRAMES, COLS), lambda i: (i, 0, 0)),
        scratch_shapes=[pltpu.VMEM((FRAMES, D_DEP), BF)],
    )(returned, target, active, text_grad[0], all_weights)
    out_grad = exchange(out_grad, "seq").reshape(LENGTH, COLS)
    grads = call(
        backward_kernel, jax.ShapeDtypeStruct((LENGTH, 3 * COLS), BF), "attention_backward"
    )(packed, out_grad)
    grads = exchange(grads.reshape(SEQ, FRAMES, 3 * COLS), "seq")
    shape = jax.ShapeDtypeStruct((FRAMES, D_CTX), BF)
    query_grad, key_grad, value_grad = call(unpack_kernel, (shape, shape, shape), "unpack_grads")(grads)
    return query_grad[None], key_grad[None], value_grad[None]


def solution(mesh):
    split = Mesh(mesh.devices.reshape(SEQ, 4, 16), ("seq", "y", "z"))
    rows = P(("y", "z"), "seq", None)
    frames = P(("y", "z"), "seq")
    code_rows = P(("y", "z"), "seq", None, None)
    flat = P(("seq", "y", "z"))
    in_specs = (
        rows,
        rows,
        rows,
        rows,
        frames,
        frames,
        code_rows,
        code_rows,
        flat,
        P(),
        flat,
        flat,
    )
    return jax.shard_map(
        shards, mesh=split, in_specs=in_specs, out_specs=(rows, rows, rows), check_vma=False
    )
```

```python
import jax
import jax.numpy as jnp
from jax import lax
from jax.experimental import pallas as pl
from jax.experimental.pallas import tpu as pltpu
from jax.sharding import Mesh
from jax.sharding import PartitionSpec as P

HEADS = 16
HEAD = 128
D_DEP = 1024
DHEADS = 8
DHEAD = 64
CODES = 8
D_CTX = 2048
FRAMES = 64
SEQ = 8
OWNERS = 64
CAP = 2
SLOTS = OWNERS * CAP
RECEIVED = 59
LENGTH = SEQ * FRAMES
COLS = D_CTX // SEQ
ROWS = RECEIVED * CODES
PADDED = 512
CHUNK = 256
GROUP = 128
EMPTY = 2.0**100
SHIFTS = (0, 1, 3, 2)
BF = jnp.bfloat16
F32 = jnp.float32


def dot(a, b):
    return jnp.dot(a, b, preferred_element_type=F32)


def dot_nt(a, b):
    return lax.dot_general(a, b, (((1,), (1,)), ((), ())), preferred_element_type=F32)


def dot_tn(a, b):
    return lax.dot_general(a, b, (((0,), (0,)), ((), ())), preferred_element_type=F32)


def iota(shape, axis):
    return lax.broadcasted_iota(jnp.int32, shape, axis)


def call(kernel, out_shape, name, **options):
    limit = options.pop("vmem", 32)
    return pl.pallas_call(
        kernel,
        out_shape=out_shape,
        name=name,
        compiler_params=pltpu.CompilerParams(vmem_limit_bytes=limit * 2**20),
        **options,
    )


def weight_kernel(*refs):
    pieces, in_ref, rest_ref, gathered_ref = refs[:4], refs[4], refs[5], refs[6]
    here = lax.axis_index("y")
    for shift, piece in zip(SHIFTS, pieces):
        start = pl.multiple_of(((here + 4 - shift) & 3) * 128, 128)
        gathered_ref[pl.ds(start, 128), :] = piece[...]
    row = iota((512, 512), 0)
    col = iota((512, 512), 1)
    none = jnp.full((512, 512), -1, jnp.int32)

    def pick(first, second, third, fourth):
        source = jnp.where(
            row < 256, first, jnp.where(row < 384, second, jnp.where(row < 448, third, fourth))
        )
        return (col == source).astype(F32).astype(BF)

    in_row = ((row >> 2) << 3) + (row & 3)
    wide = row - 256
    wide_base = (wide >> 1) << 3
    wide_odd = (wide & 1) == 1
    tail = row - 384
    tail_base = (tail >> 1) << 3
    tail_odd = (tail & 1) == 1
    out_row = ((row - 448) << 3) + 7
    left_left = pick(
        in_row,
        jnp.where(wide_odd, none, wide_base + 4),
        jnp.where(tail_odd, none, tail_base + 5),
        out_row,
    )
    left_right = pick(
        none, jnp.where(wide_odd, wide_base + 5, none), jnp.where(tail_odd, tail_base + 6, none), none
    )
    right_left = pick(
        none,
        jnp.where(wide_odd, wide_base + 6, none),
        jnp.where(tail_odd, none, tail_base + 256 + 5),
        none,
    )
    right_right = pick(
        in_row,
        jnp.where(wide_odd, none, wide_base + 4),
        jnp.where(tail_odd, tail_base + 256 + 6, none),
        out_row,
    )
    left = gathered_ref[:, :512]
    right = gathered_ref[:, 512:]
    new_left = (dot(left_left, left) + dot(left_right, right)).astype(BF)
    new_right = (dot(right_left, left) + dot(right_right, right)).astype(BF)
    for ref, rows in ((in_ref, slice(0, 256)), (rest_ref, slice(256, 512))):
        ref[:, :512] = new_left[rows]
        ref[:, 512:] = new_right[rows]


def pack_kernel(first_ref, second_ref, third_ref, out_ref):
    for part in range(SEQ):
        for place, ref in enumerate((first_ref, second_ref, third_ref)):
            out_ref[part, :, place * COLS : (place + 1) * COLS] = ref[
                :, part * COLS : (part + 1) * COLS
            ]


def unpack_kernel(packed_ref, first_ref, second_ref, third_ref):
    for part in range(SEQ):
        for place, ref in enumerate((first_ref, second_ref, third_ref)):
            ref[:, part * COLS : (part + 1) * COLS] = packed_ref[
                part, :, place * COLS : (place + 1) * COLS
            ]


def head_weights(packed_ref, head):
    base = head * HEAD
    query = packed_ref[:, base : base + HEAD]
    key = packed_ref[:, COLS + base : COLS + base + HEAD]
    value = packed_ref[:, 2 * COLS + base : 2 * COLS + base + HEAD]
    scores = dot_nt(query, key) * HEAD ** (-0.5)
    allowed = iota((LENGTH, LENGTH), 1) <= iota((LENGTH, LENGTH), 0)
    scores = jnp.where(allowed, scores, -1e30)
    raised = jnp.exp(scores - jnp.max(scores, axis=1, keepdims=True))
    weights = raised * (1.0 / jnp.sum(raised, axis=1, keepdims=True))
    return query, key, value, weights


def forward_kernel(packed_ref, w_in_ref, out_ref):
    total = None
    for head in range(2):
        unused_q, unused_k, value, weights = head_weights(packed_ref, head)
        context = dot(weights.astype(BF), value).astype(BF)
        part = dot(context, w_in_ref[head * HEAD : (head + 1) * HEAD, :])
        total = part if total is None else total + part
    out_ref[...] = total.astype(BF)


def backward_kernel(packed_ref, grad_ref, out_ref):
    for head in range(2):
        base = head * HEAD
        query, key, value, weights = head_weights(packed_ref, head)
        grad = grad_ref[:, base : base + HEAD]
        weight_grad = dot_nt(grad, value).astype(BF).astype(F32)
        inner = jnp.sum(weight_grad * weights, axis=1, keepdims=True)
        score_grad = (weights * (weight_grad - inner) * HEAD ** (-0.5)).astype(BF)
        out_ref[:, base : base + HEAD] = dot(score_grad, key).astype(BF)
        out_ref[:, COLS + base : COLS + base + HEAD] = dot_tn(score_grad, query).astype(BF)
        out_ref[:, 2 * COLS + base : 2 * COLS + base + HEAD] = dot_tn(
            weights.astype(BF), grad
        ).astype(BF)


def routing(target_ref, active_ref):
    down = iota((FRAMES, FRAMES), 0)
    across = iota((FRAMES, FRAMES), 1)
    target_row = target_ref[...].astype(F32)
    live_row = (active_ref[...] == 1).astype(F32)
    target_col = jnp.sum(jnp.where(down == across, target_row, 0.0), axis=1, keepdims=True)
    live_col = jnp.sum(jnp.where(down == across, live_row, 0.0), axis=1, keepdims=True)
    same = target_col == target_row
    earlier_row = jnp.sum(jnp.where(same & (down < across), live_col, 0.0), axis=0, keepdims=True)
    earlier_col = jnp.sum(jnp.where(same & (across < down), live_row, 0.0), axis=1, keepdims=True)
    return (target_row, live_row, earlier_row), (target_col, live_col, earlier_col)


def send_kernel(parts_ref, target_ref, active_ref, out_ref):
    rows = parts_ref[0].astype(F32)
    for part in range(1, SEQ):
        rows = rows + parts_ref[part].astype(F32)
    (target, live, earlier), unused = routing(target_ref, active_ref)
    slot = iota((SLOTS, FRAMES), 0)
    chosen = (
        (target == (slot >> 1).astype(F32)) & (live > 0.5) & (earlier == (slot & 1).astype(F32))
    ).astype(F32)
    sent = dot(chosen.astype(BF), rows.astype(BF))
    filled = jnp.sum(chosen, axis=1, keepdims=True) > 0.5
    out_ref[...] = jnp.where(filled, sent, EMPTY).astype(BF)


def parts_held():
    x, core = lax.axis_index("x"), lax.axis_index("core")
    return [((x + 4 - shift) & 3) * 2 + side for side in (core, 1 - core) for shift in SHIFTS]


def return_kernel(returned_ref, target_ref, active_ref, text_ref, *refs):
    pieces, out_ref = refs[:SEQ], refs[SEQ]
    unused, (target, live, earlier) = routing(target_ref, active_ref)
    slot = iota((FRAMES, SLOTS), 1)
    chosen = (
        (target == (slot >> 1).astype(F32)) & (live > 0.5) & (earlier == (slot & 1).astype(F32))
    ).astype(F32)
    rows = dot(chosen.astype(BF), returned_ref[...]).astype(BF)
    for part, piece in zip(parts_held(), pieces):
        carried = dot_nt(rows, piece[...]).astype(BF).astype(F32)
        start = pl.multiple_of(part * COLS, COLS)
        out_ref[part] = (text_ref[:, pl.ds(start, COLS)].astype(F32) + carried).astype(BF)


def depth_kernel(slots_ref, codes_ref, cot_ref, gain_ref, *refs):
    pieces, refs = refs[:SEQ], refs[SEQ:]
    out_ref, w_qkv, w_out, hidden_s, cot_s, grads_s, frames_s, sems = refs
    copies = []
    for part, piece in zip(parts_held(), pieces):
        low = pl.multiple_of(part * 128, 128)
        low_half = pl.multiple_of(part * 64, 64)
        pairs = (
            (piece.at[:128, :], w_qkv.at[pl.ds(low, 128), :1024]),
            (piece.at[128:192, :512], w_qkv.at[pl.ds(low, 64), 1024:]),
            (piece.at[128:192, 512:], w_qkv.at[pl.ds(low + 64, 64), 1024:]),
            (piece.at[192:256, :], w_out.at[pl.ds(low_half, 64), :]),
        )
        for source, goal in pairs:
            copies.append(pltpu.make_async_copy(source, goal, sems.at[len(copies)]))
    for copy in copies:
        copy.start()

    slots = slots_ref[...]
    live_col = (slots[:, 0:1].astype(F32) < EMPTY * 0.5).astype(F32)
    down = iota((SLOTS, SLOTS), 0)
    across = iota((SLOTS, SLOTS), 1)
    live_row = jnp.sum(jnp.where(down == across, live_col, 0.0), axis=0, keepdims=True)
    rank_row = jnp.sum(jnp.where(down < across, live_col, 0.0), axis=0, keepdims=True)
    rank_col = jnp.sum(jnp.where(across < down, live_row, 0.0), axis=1, keepdims=True)

    spread = (
        (live_row > 0.5) & (rank_row == (iota((PADDED, SLOTS), 0) >> 3).astype(F32))
    ).astype(F32)
    spare = jnp.zeros((PADDED - ROWS, D_DEP), F32)
    hidden_s[...] = dot(spread.astype(BF), slots) + jnp.concatenate(
        [codes_ref[...].astype(F32), spare], axis=0
    )
    cot_s[...] = jnp.concatenate([cot_ref[...].astype(F32), spare], axis=0)
    gain = gain_ref[...].astype(F32)
    for copy in copies:
        copy.wait()

    row = iota((GROUP, GROUP), 0)
    col = iota((GROUP, GROUP), 1)
    allowed = ((row >> 3) == (col >> 3)) & (col <= row)
    first_half = iota((GROUP, GROUP), 1) < DHEAD
    nothing = jnp.zeros((GROUP, GROUP), BF)
    width = DHEADS * DHEAD
    for chunk in range(PADDED // CHUNK):
        low = chunk * CHUNK
        hidden = hidden_s[low : low + CHUNK, :]
        cot = cot_s[low : low + CHUNK, :]
        scale = lax.rsqrt(jnp.sum(hidden * hidden, axis=1, keepdims=True) * (1.0 / D_DEP) + 1e-05)
        normed = (hidden * scale * gain).astype(BF)
        projected = dot(normed, w_qkv[...]).astype(BF)
        mixed_grad = dot_nt(cot.astype(BF), w_out[...]).astype(BF)
        for group in range(CHUNK // GROUP):
            rows = slice(group * GROUP, (group + 1) * GROUP)
            for pair in range(DHEADS // 2):
                lanes = pair * 128
                query = projected[rows, lanes : lanes + 128]
                key = projected[rows, width + lanes : width + lanes + 128]
                value = projected[rows, 2 * width + lanes : 2 * width + lanes + 128]
                grad = mixed_grad[rows, lanes : lanes + 128]
                totals = [None, None, None]
                for half in range(2):
                    own = first_half if half == 0 else ~first_half
                    own_query = jnp.where(own, query, nothing)
                    own_key = jnp.where(own, key, nothing)
                    own_grad = jnp.where(own, grad, nothing)
                    scores = dot_nt(own_query, key) * DHEAD ** (-0.5)
                    scores = jnp.where(allowed, scores, -1e30)
                    raised = jnp.exp(scores - jnp.max(scores, axis=1, keepdims=True))
                    weights = raised * (1.0 / jnp.sum(raised, axis=1, keepdims=True))
                    weight_grad = dot_nt(own_grad, value).astype(BF).astype(F32)
                    inner = jnp.sum(weight_grad * weights, axis=1, keepdims=True)
                    score_grad = (weights * (weight_grad - inner) * DHEAD ** (-0.5)).astype(BF)
                    terms = (
                        dot(score_grad, own_key),
                        dot_tn(score_grad, own_query),
                        dot_tn(weights.astype(BF), own_grad),
                    )
                    totals = [t if s is None else s + t for s, t in zip(totals, terms)]
                for place, total in enumerate(totals):
                    start = place * width + lanes
                    grads_s[rows, start : start + 128] = total.astype(BF)
        normed_grad = dot_nt(grads_s[...], w_qkv[...]).astype(BF).astype(F32) * gain
        inner = jnp.sum(normed_grad * hidden, axis=1, keepdims=True) * (1.0 / D_DEP)
        hidden_grad = cot + scale * normed_grad - hidden * (scale * scale * scale * inner)
        frames = jnp.sum(hidden_grad.reshape(CHUNK // CODES, CODES, D_DEP), axis=1)
        frames_s[low // CODES : (low + CHUNK) // CODES, :] = frames

    back = ((live_col > 0.5) & (rank_col == iota((SLOTS, FRAMES), 1).astype(F32))).astype(F32)
    out_ref[...] = dot(back.astype(BF), frames_s[...].astype(BF)).astype(BF)


def exchange(array, axis):
    return lax.all_to_all(array, axis, split_axis=0, concat_axis=0, tiled=True)


def moved(array, axis, size, shift):
    return lax.ppermute(array, axis, [(i, (i + shift) % size) for i in range(size)])


def gathered(piece):
    along = [piece] + [moved(piece, "x", 4, shift) for shift in SHIFTS[1:]]
    return along + [moved(each, "core", 2, 1) for each in along]


def shards(
    queries,
    keys,
    values,
    text_grad,
    active,
    target,
    codes,
    depth_cot,
    w_in,
    norm_gain,
    w_qkv,
    w_out,
):
    seq = ("x", "core")
    owner = ("y", "z")
    mine = jnp.concatenate([w_in, w_qkv, w_out]).reshape(1, 8, D_DEP)
    along_z = exchange(jnp.broadcast_to(mine, (16, 8, D_DEP)), "z").reshape(128, D_DEP)
    along_y = [along_z] + [moved(along_z, "y", 4, shift) for shift in SHIFTS[1:]]
    half = jax.ShapeDtypeStruct((256, D_DEP), BF)
    own_in, own_rest = call(
        weight_kernel,
        (half, half),
        "sort_weights",
        scratch_shapes=[pltpu.VMEM((512, D_DEP), BF)],
    )(*along_y)
    rest = gathered(own_rest)

    packed = call(pack_kernel, jax.ShapeDtypeStruct((SEQ, FRAMES, 3 * COLS), BF), "pack_qkv")(
        queries[0], keys[0], values[0]
    )
    packed = exchange(packed, seq).reshape(LENGTH, 3 * COLS)
    parts = call(
        forward_kernel,
        jax.ShapeDtypeStruct((LENGTH, D_DEP), BF),
        "attention_forward",
    )(packed, own_in)
    parts = exchange(parts.reshape(SEQ, FRAMES, D_DEP), seq)
    late_in, unused = lax.optimization_barrier((own_in, parts))
    all_in = gathered(late_in)
    sent = call(send_kernel, jax.ShapeDtypeStruct((SLOTS, D_DEP), BF), "send_rows")(
        parts, target, active
    )
    slots = exchange(sent.reshape(OWNERS, CAP, D_DEP), owner).reshape(SLOTS, D_DEP)
    vmem = pl.BlockSpec(memory_space=pltpu.VMEM)
    grads = call(
        depth_kernel,
        jax.ShapeDtypeStruct((SLOTS, D_DEP), BF),
        "depth_layer",
        in_specs=[vmem] * 4 + [pl.BlockSpec(memory_space=pl.ANY)] * SEQ,
        out_specs=vmem,
        scratch_shapes=[
            pltpu.VMEM((D_DEP, 3 * DHEADS * DHEAD), BF),
            pltpu.VMEM((DHEADS * DHEAD, D_DEP), BF),
            pltpu.VMEM((PADDED, D_DEP), F32),
            pltpu.VMEM((PADDED, D_DEP), F32),
            pltpu.VMEM((CHUNK, 3 * DHEADS * DHEAD), BF),
            pltpu.VMEM((FRAMES, D_DEP), F32),
            pltpu.SemaphoreType.DMA((4 * SEQ,)),
        ],
        vmem=48,
    )(
        slots,
        codes.reshape(ROWS, D_DEP),
        depth_cot.reshape(ROWS, D_DEP),
        norm_gain.reshape(1, D_DEP),
        *rest,
    )
    returned = exchange(grads.reshape(OWNERS, CAP, D_DEP), owner).reshape(SLOTS, D_DEP)
    out_grad = call(
        return_kernel,
        jax.ShapeDtypeStruct((SEQ, FRAMES, COLS), BF),
        "return_rows",
    )(returned, target, active, text_grad[0], *all_in)
    out_grad = exchange(out_grad, seq).reshape(LENGTH, COLS)
    grads = call(
        backward_kernel, jax.ShapeDtypeStruct((LENGTH, 3 * COLS), BF), "attention_backward"
    )(packed, out_grad)
    grads = exchange(grads.reshape(SEQ, FRAMES, 3 * COLS), seq)
    shape = jax.ShapeDtypeStruct((FRAMES, D_CTX), BF)
    query_grad, key_grad, value_grad = call(unpack_kernel, (shape, shape, shape), "unpack_grads")(grads)
    return query_grad[None], key_grad[None], value_grad[None]


def solution(mesh):
    split = Mesh(mesh.devices.reshape(4, 2, 4, 16), ("x", "core", "y", "z"))
    rows = P(("y", "z"), ("x", "core"), None)
    frames = P(("y", "z"), ("x", "core"))
    code_rows = P(("y", "z"), ("x", "core"), None, None)
    flat = P(("x", "core", "y", "z"))
    in_specs = (
        rows,
        rows,
        rows,
        rows,
        frames,
        frames,
        code_rows,
        code_rows,
        flat,
        P(),
        flat,
        flat,
    )
    return jax.shard_map(
        shards, mesh=split, in_specs=in_specs, out_specs=(rows, rows, rows), check_vma=False
    )
```

```python
import jax
import jax.numpy as jnp
from jax import lax
from jax.experimental import pallas as pl
from jax.experimental.pallas import tpu as pltpu
from jax.sharding import Mesh
from jax.sharding import PartitionSpec as P

HEADS = 16
HEAD = 128
D_DEP = 1024
DHEADS = 8
DHEAD = 64
CODES = 8
D_CTX = 2048
FRAMES = 64
SEQ = 8
OWNERS = 64
CAP = 2
SLOTS = OWNERS * CAP
RECEIVED = 59
LENGTH = SEQ * FRAMES
COLS = D_CTX // SEQ
ROWS = RECEIVED * CODES
PADDED = 512
GROUP = 128
EMPTY = 2.0**100
SHIFTS = (0, 1, 3, 2)
BF = jnp.bfloat16
F32 = jnp.float32


def dot(a, b):
    return jnp.dot(a, b, preferred_element_type=F32)


def dot_nt(a, b):
    return lax.dot_general(a, b, (((1,), (1,)), ((), ())), preferred_element_type=F32)


def dot_tn(a, b):
    return lax.dot_general(a, b, (((0,), (0,)), ((), ())), preferred_element_type=F32)


def iota(shape, axis):
    return lax.broadcasted_iota(jnp.int32, shape, axis)


def call(kernel, out_shape, name, **options):
    limit = options.pop("vmem", 32)
    return pl.pallas_call(
        kernel,
        out_shape=out_shape,
        name=name,
        compiler_params=pltpu.CompilerParams(vmem_limit_bytes=limit * 2**20),
        **options,
    )


def weight_kernel(*refs):
    pieces, in_ref, rest_ref, gathered_ref = refs[:4], refs[4], refs[5], refs[6]
    here = lax.axis_index("y")
    for shift, piece in zip(SHIFTS, pieces):
        start = pl.multiple_of(((here + 4 - shift) & 3) * 128, 128)
        gathered_ref[pl.ds(start, 128), :] = piece[...]

    def picked(rows, source):
        return (iota((rows, 512), 1) == source).astype(F32).astype(BF)

    row = iota((256, 512), 0)
    in_ref[...] = dot(picked(256, ((row >> 2) << 3) + (row & 3)), gathered_ref[...]).astype(BF)
    row = iota((128, 512), 0)
    base = (row >> 1) << 3
    even = (row & 1) == 0
    upper = row < 64
    wanted = (
        (jnp.where(even, base + 4, -1), jnp.where(even, -1, base + 5)),
        (jnp.where(even, -1, base + 6), jnp.where(even, base + 4, -1)),
        (jnp.where(even, base + 5, -1), jnp.where(even, -1, base + 6)),
        (jnp.where(upper, (row << 3) + 7, -1), jnp.where(upper, -1, ((row - 64) << 3) + 7)),
    )
    left = gathered_ref[:, :512]
    right = gathered_ref[:, 512:]
    for place, (from_left, from_right) in enumerate(wanted):
        new = dot(picked(128, from_left), left) + dot(picked(128, from_right), right)
        rest_ref[:, place * 512 : (place + 1) * 512] = new.astype(BF)


def pack_kernel(*refs):
    ins, out_ref = refs[:4], refs[4]
    for part in range(SEQ):
        for place, ref in enumerate(ins):
            out_ref[part, :, place * COLS : (place + 1) * COLS] = ref[
                :, part * COLS : (part + 1) * COLS
            ]


def unpack_kernel(packed_ref, first_ref, second_ref, third_ref):
    for part in range(SEQ):
        for place, ref in enumerate((first_ref, second_ref, third_ref)):
            ref[:, part * COLS : (part + 1) * COLS] = packed_ref[
                part, :, place * COLS : (place + 1) * COLS
            ]


def head_weights(packed_ref, head):
    base = head * HEAD
    query = packed_ref[:, base : base + HEAD]
    key = packed_ref[:, COLS + base : COLS + base + HEAD]
    value = packed_ref[:, 2 * COLS + base : 2 * COLS + base + HEAD]
    scores = dot_nt(query, key) * HEAD ** (-0.5)
    allowed = iota((LENGTH, LENGTH), 1) <= iota((LENGTH, LENGTH), 0)
    scores = jnp.where(allowed, scores, -1e30)
    raised = jnp.exp(scores - jnp.max(scores, axis=1, keepdims=True))
    weights = raised * (1.0 / jnp.sum(raised, axis=1, keepdims=True))
    return query, key, value, weights


def forward_kernel(packed_ref, w_in_ref, out_ref):
    total = None
    for head in range(2):
        unused_q, unused_k, value, weights = head_weights(packed_ref, head)
        context = dot(weights.astype(BF), value).astype(BF)
        part = dot(context, w_in_ref[head * HEAD : (head + 1) * HEAD, :])
        total = part if total is None else total + part
    out_ref[...] = total.astype(BF)


def backward_kernel(packed_ref, own_ref, near_ref, out_ref, grad_s):
    core = lax.axis_index("core")
    for x in range(4):
        for side, ref in ((core, own_ref), (1 - core, near_ref)):
            start = pl.multiple_of((2 * x + side) * FRAMES, FRAMES)
            carried = ref[x * FRAMES : (x + 1) * FRAMES, :].astype(F32)
            text = packed_ref[pl.ds(start, FRAMES), 3 * COLS :].astype(F32)
            grad_s[pl.ds(start, FRAMES), :] = (text + carried).astype(BF)
    for head in range(2):
        base = head * HEAD
        query, key, value, weights = head_weights(packed_ref, head)
        grad = grad_s[:, base : base + HEAD]
        weight_grad = dot_nt(grad, value).astype(BF).astype(F32)
        inner = jnp.sum(weight_grad * weights, axis=1, keepdims=True)
        score_grad = (weights * (weight_grad - inner) * HEAD ** (-0.5)).astype(BF)
        out_ref[:, base : base + HEAD] = dot(score_grad, key).astype(BF)
        out_ref[:, COLS + base : COLS + base + HEAD] = dot_tn(score_grad, query).astype(BF)
        out_ref[:, 2 * COLS + base : 2 * COLS + base + HEAD] = dot_tn(
            weights.astype(BF), grad
        ).astype(BF)


def routing(target_ref, active_ref):
    down = iota((FRAMES, FRAMES), 0)
    across = iota((FRAMES, FRAMES), 1)
    target_row = target_ref[...].astype(F32)
    live_row = (active_ref[...] == 1).astype(F32)
    target_col = jnp.sum(jnp.where(down == across, target_row, 0.0), axis=1, keepdims=True)
    live_col = jnp.sum(jnp.where(down == across, live_row, 0.0), axis=1, keepdims=True)
    same = target_col == target_row
    earlier_row = jnp.sum(jnp.where(same & (down < across), live_col, 0.0), axis=0, keepdims=True)
    earlier_col = jnp.sum(jnp.where(same & (across < down), live_row, 0.0), axis=1, keepdims=True)
    return (target_row, live_row, earlier_row), (target_col, live_col, earlier_col)


def narrow_to_wide(narrow_ref, scratch):
    scratch[...] = narrow_ref[...].astype(F32)
    return jnp.concatenate([scratch[pl.ds(c, SLOTS, stride=8), :] for c in range(8)], axis=1)


def wide_to_narrow(wide, narrow_ref, scratch):
    for c in range(8):
        scratch[pl.ds(c, SLOTS, stride=8), :] = wide[:, c * 128 : (c + 1) * 128]
    narrow_ref[...] = scratch[...].astype(BF)


def send_kernel(parts_ref, target_ref, active_ref, out_ref, narrow_s):
    rows = parts_ref[0].astype(F32)
    for part in range(1, SEQ):
        rows = rows + parts_ref[part].astype(F32)
    (target, live, earlier), unused = routing(target_ref, active_ref)
    slot = iota((SLOTS, FRAMES), 0)
    chosen = (
        (target == (slot >> 1).astype(F32)) & (live > 0.5) & (earlier == (slot & 1).astype(F32))
    ).astype(F32)
    sent = dot(chosen.astype(BF), rows.astype(BF))
    filled = jnp.sum(chosen, axis=1, keepdims=True) > 0.5
    wide_to_narrow(jnp.where(filled, sent, EMPTY), out_ref, narrow_s)


def parts_held():
    x, core = lax.axis_index("x"), lax.axis_index("core")
    return [((x + 4 - shift) & 3) * 2 + side for side in (core, 1 - core) for shift in SHIFTS]


def return_kernel(returned_ref, target_ref, active_ref, out_ref, narrow_s):
    unused, (target, live, earlier) = routing(target_ref, active_ref)
    slot = iota((FRAMES, SLOTS), 1)
    chosen = (
        (target == (slot >> 1).astype(F32)) & (live > 0.5) & (earlier == (slot & 1).astype(F32))
    ).astype(F32)
    returned = narrow_to_wide(returned_ref, narrow_s).astype(BF)
    rows = dot(chosen.astype(BF), returned).astype(BF)
    for x in range(4):
        out_ref[x] = rows


def carry_kernel(rows_ref, own_in_ref, near_in_ref, own_ref, near_ref):
    own_ref[...] = dot_nt(rows_ref[...], own_in_ref[...]).astype(BF)
    near_ref[...] = dot_nt(rows_ref[...], near_in_ref[...]).astype(BF)


def depth_kernel(slots_ref, codes_ref, cot_ref, gain_ref, *refs):
    pieces, refs = refs[:SEQ], refs[SEQ:]
    (
        out_ref,
        weights_s,
        hidden_s,
        cot_s,
        mixed_s,
        projected_s,
        grads_s,
        narrow_s,
        codes_s,
        given_s,
        sems,
    ) = refs
    copies = [
        pltpu.make_async_copy(codes_ref, codes_s, sems.at[0]),
        pltpu.make_async_copy(cot_ref, given_s, sems.at[1]),
    ]
    for part, piece in zip(parts_held(), pieces):
        goal = weights_s.at[pl.ds(pl.multiple_of(part * 128, 128), 128), :]
        copies.append(pltpu.make_async_copy(piece, goal, sems.at[len(copies)]))
    for copy in copies:
        copy.start()

    slots = narrow_to_wide(slots_ref, narrow_s).astype(BF)
    live_col = (slots[:, 0:1].astype(F32) < EMPTY * 0.5).astype(F32)
    down = iota((SLOTS, SLOTS), 0)
    across = iota((SLOTS, SLOTS), 1)
    live_row = jnp.sum(jnp.where(down == across, live_col, 0.0), axis=0, keepdims=True)
    rank_row = jnp.sum(jnp.where(down < across, live_col, 0.0), axis=0, keepdims=True)
    rank_col = jnp.sum(jnp.where(across < down, live_row, 0.0), axis=1, keepdims=True)

    spread = (
        (live_row > 0.5) & (rank_row == (iota((PADDED, SLOTS), 0) >> 3).astype(F32))
    ).astype(F32)
    spare = jnp.zeros((PADDED - ROWS, D_DEP), F32)
    copies[0].wait()
    hidden = dot(spread.astype(BF), slots) + jnp.concatenate(
        [codes_s[...].astype(F32), spare], axis=0
    )
    hidden_s[...] = hidden
    copies[1].wait()
    cot_s[...] = jnp.concatenate([given_s[...].astype(F32), spare], axis=0)
    gain = gain_ref[...].astype(F32)
    scale = lax.rsqrt(jnp.sum(hidden * hidden, axis=1, keepdims=True) * (1.0 / D_DEP) + 1e-05)
    normed = (hidden * scale * gain).astype(BF)
    for copy in copies[2:]:
        copy.wait()
    width = DHEADS * DHEAD
    w_out = weights_s[:, 3 * width :].reshape(SEQ, 2, DHEAD, width)
    mixed_grad = dot_nt(cot_s[:, :width].astype(BF), w_out[:, 0].reshape(width, width))
    mixed_grad += dot_nt(cot_s[:, width:].astype(BF), w_out[:, 1].reshape(width, width))
    mixed_s[...] = mixed_grad.astype(BF)
    projected_s[...] = dot(normed, weights_s[:, : 3 * width]).astype(BF)

    first_half = iota((GROUP, 128), 1) < DHEAD
    nothing = jnp.zeros((GROUP, 128), BF)
    frame = iota((GROUP // CODES, CODES, 2 * GROUP), 0)
    row = iota((GROUP // CODES, CODES, 2 * GROUP), 2) & (GROUP - 1)
    same_frame = frame == (row >> 3)

    def halves(array):
        return jnp.concatenate(
            [jnp.where(first_half, array, nothing), jnp.where(first_half, nothing, array)], axis=0
        )

    def own_frame(array):
        blocks = array.reshape(GROUP // CODES, CODES, 2 * GROUP)
        return jnp.sum(jnp.where(same_frame, blocks, 0.0), axis=0)

    def all_frames(array):
        blocks = jnp.where(same_frame, array[None], 0.0)
        return blocks.reshape(GROUP, 2 * GROUP).astype(BF)

    units = [
        (slice(group * GROUP, (group + 1) * GROUP), pair * 128)
        for group in range(PADDED // GROUP)
        for pair in range(DHEADS // 2)
    ]
    scores, weight_grad = [], []
    for rows, lanes in units:
        key = projected_s[rows, width + lanes : width + lanes + 128]
        value = projected_s[rows, 2 * width + lanes : 2 * width + lanes + 128]
        scores.append(own_frame(dot_nt(key, halves(projected_s[rows, lanes : lanes + 128]))))
        weight_grad.append(own_frame(dot_nt(value, halves(mixed_s[rows, lanes : lanes + 128]))))
    scores = jnp.concatenate(scores, axis=1) * DHEAD ** (-0.5)
    scores = jnp.where((iota(scores.shape, 0) <= (iota(scores.shape, 1) & 7)), scores, -1e30)
    raised = jnp.exp(scores - jnp.max(scores, axis=0, keepdims=True))
    weights = raised * (1.0 / jnp.sum(raised, axis=0, keepdims=True))
    weight_grad = jnp.concatenate(weight_grad, axis=1).astype(BF).astype(F32)
    inner = jnp.sum(weight_grad * weights, axis=0, keepdims=True)
    score_grad = weights * (weight_grad - inner) * DHEAD ** (-0.5)
    for place, (rows, lanes) in enumerate(units):
        own = slice(place * 2 * GROUP, (place + 1) * 2 * GROUP)
        back = all_frames(score_grad[:, own])
        query_grad = dot_tn(back, projected_s[rows, width + lanes : width + lanes + 128])
        grads_s[rows, lanes : lanes + 128] = jnp.where(
            first_half, query_grad[:GROUP], query_grad[GROUP:]
        ).astype(BF)
        grads_s[rows, width + lanes : width + lanes + 128] = dot(
            back, halves(projected_s[rows, lanes : lanes + 128])
        ).astype(BF)
        grads_s[rows, 2 * width + lanes : 2 * width + lanes + 128] = dot(
            all_frames(weights[:, own]), halves(mixed_s[rows, lanes : lanes + 128])
        ).astype(BF)
    normed_grad = dot_nt(grads_s[...], weights_s[:, : 3 * width]).astype(BF).astype(F32) * gain
    hidden = hidden_s[...]
    inner = jnp.sum(normed_grad * hidden, axis=1, keepdims=True) * (1.0 / D_DEP)
    hidden_grad = cot_s[...] + scale * normed_grad - hidden * (scale * scale * scale * inner)
    frames = jnp.sum(hidden_grad.reshape(FRAMES, CODES, D_DEP), axis=1)

    back = ((live_col > 0.5) & (rank_col == iota((SLOTS, FRAMES), 1).astype(F32))).astype(F32)
    wide_to_narrow(dot(back.astype(BF), frames.astype(BF)), out_ref, narrow_s)


def depth_scratch():
    width = DHEADS * DHEAD
    return [
        pltpu.VMEM((D_DEP, 4 * width), BF),
        pltpu.VMEM((PADDED, D_DEP), F32),
        pltpu.VMEM((PADDED, D_DEP), F32),
        pltpu.VMEM((PADDED, width), BF),
        pltpu.VMEM((PADDED, 3 * width), BF),
        pltpu.VMEM((PADDED, 3 * width), BF),
        pltpu.VMEM((SLOTS * 8, 128), F32),
        pltpu.VMEM((ROWS, D_DEP), BF),
        pltpu.VMEM((ROWS, D_DEP), BF),
        pltpu.SemaphoreType.DMA((SEQ + 2,)),
    ]


def exchange(array, axis):
    return lax.all_to_all(array, axis, split_axis=0, concat_axis=0, tiled=True)


def moved(array, axis, size, shift):
    return lax.ppermute(array, axis, [(i, (i + shift) % size) for i in range(size)])


def shards(
    queries,
    keys,
    values,
    text_grad,
    active,
    target,
    codes,
    depth_cot,
    w_in,
    norm_gain,
    w_qkv,
    w_out,
):
    seq = ("x", "core")
    owner = ("y", "z")
    mine = jnp.concatenate([w_in, w_qkv, w_out]).reshape(1, 8, D_DEP)
    along_z = exchange(jnp.broadcast_to(mine, (16, 8, D_DEP)), "z").reshape(128, D_DEP)
    along_y = [along_z] + [moved(along_z, "y", 4, shift) for shift in SHIFTS[1:]]
    own_in, own_rest = call(
        weight_kernel,
        (jax.ShapeDtypeStruct((256, D_DEP), BF), jax.ShapeDtypeStruct((128, 2 * D_DEP), BF)),
        "sort_weights",
        scratch_shapes=[pltpu.VMEM((512, D_DEP), BF)],
    )(*along_y)
    rest = [own_rest] + [moved(own_rest, "x", 4, shift) for shift in SHIFTS[1:]]
    rest += [moved(piece, "core", 2, 1) for piece in rest]

    packed = call(pack_kernel, jax.ShapeDtypeStruct((SEQ, FRAMES, 4 * COLS), BF), "pack_heads")(
        queries[0], keys[0], values[0], text_grad[0]
    )
    packed = exchange(packed, seq).reshape(LENGTH, 4 * COLS)
    parts = call(
        forward_kernel,
        jax.ShapeDtypeStruct((LENGTH, D_DEP), BF),
        "attention_forward",
    )(packed, own_in)
    parts = exchange(parts.reshape(SEQ, FRAMES, D_DEP), seq)
    narrow = jax.ShapeDtypeStruct((SLOTS * 8, 128), BF)
    sent = call(
        send_kernel, narrow, "send_rows", scratch_shapes=[pltpu.VMEM((SLOTS * 8, 128), F32)]
    )(parts, target, active)
    slots = exchange(sent.reshape(OWNERS, 16, 128), owner).reshape(SLOTS * 8, 128)
    vmem = pl.BlockSpec(memory_space=pltpu.VMEM)
    anywhere = pl.BlockSpec(memory_space=pl.ANY)
    grads = call(
        depth_kernel,
        narrow,
        "depth_layer",
        in_specs=[vmem, anywhere, anywhere, vmem] + [anywhere] * SEQ,
        out_specs=vmem,
        scratch_shapes=depth_scratch(),
        vmem=58,
    )(
        slots,
        codes.reshape(ROWS, D_DEP),
        depth_cot.reshape(ROWS, D_DEP),
        norm_gain.reshape(1, D_DEP),
        *rest,
    )
    late_in, unused = lax.optimization_barrier((own_in, grads))
    near_in = moved(late_in, "core", 2, 1)
    returned = exchange(grads.reshape(OWNERS, 16, 128), owner).reshape(SLOTS * 8, 128)
    rows = call(
        return_kernel,
        jax.ShapeDtypeStruct((4, FRAMES, D_DEP), BF),
        "return_rows",
        scratch_shapes=[pltpu.VMEM((SLOTS * 8, 128), F32)],
    )(returned, target, active)
    rows = exchange(rows, "x").reshape(4 * FRAMES, D_DEP)
    half = jax.ShapeDtypeStruct((4 * FRAMES, COLS), BF)
    own_carried, near_carried = call(carry_kernel, (half, half), "context_grads")(
        rows, own_in, near_in
    )
    grads = call(
        backward_kernel,
        jax.ShapeDtypeStruct((LENGTH, 3 * COLS), BF),
        "attention_backward",
        scratch_shapes=[pltpu.VMEM((LENGTH, COLS), BF)],
    )(packed, own_carried, moved(near_carried, "core", 2, 1))
    grads = exchange(grads.reshape(SEQ, FRAMES, 3 * COLS), seq)
    shape = jax.ShapeDtypeStruct((FRAMES, D_CTX), BF)
    query_grad, key_grad, value_grad = call(unpack_kernel, (shape, shape, shape), "unpack_grads")(grads)
    return query_grad[None], key_grad[None], value_grad[None]


def solution(mesh):
    split = Mesh(mesh.devices.reshape(4, 2, 4, 16), ("x", "core", "y", "z"))
    rows = P(("y", "z"), ("x", "core"), None)
    frames = P(("y", "z"), ("x", "core"))
    code_rows = P(("y", "z"), ("x", "core"), None, None)
    flat = P(("x", "core", "y", "z"))
    in_specs = (
        rows,
        rows,
        rows,
        rows,
        frames,
        frames,
        code_rows,
        code_rows,
        flat,
        P(),
        flat,
        flat,
    )
    return jax.shard_map(
        shards, mesh=split, in_specs=in_specs, out_specs=(rows, rows, rows), check_vma=False
    )
```

```python
import jax
import jax.numpy as jnp
from jax import lax
from jax.experimental import pallas as pl
from jax.experimental.pallas import tpu as pltpu
from jax.sharding import Mesh
from jax.sharding import PartitionSpec as P

HEADS = 16
HEAD = 128
D_DEP = 1024
DHEADS = 8
DHEAD = 64
CODES = 8
D_CTX = 2048
FRAMES = 64
SEQ = 8
OWNERS = 64
CAP = 2
SLOTS = OWNERS * CAP
RECEIVED = 59
LENGTH = SEQ * FRAMES
COLS = D_CTX // SEQ
ROWS = RECEIVED * CODES
PADDED = 512
GROUP = 128
EMPTY = 2.0**100
SHIFTS = (0, 1, 3, 2)
BF = jnp.bfloat16
F32 = jnp.float32


def dot(a, b):
    return jnp.dot(a, b, preferred_element_type=F32)


def dot_nt(a, b):
    return lax.dot_general(a, b, (((1,), (1,)), ((), ())), preferred_element_type=F32)


def dot_tn(a, b):
    return lax.dot_general(a, b, (((0,), (0,)), ((), ())), preferred_element_type=F32)


def iota(shape, axis):
    return lax.broadcasted_iota(jnp.int32, shape, axis)


def call(kernel, out_shape, name, **options):
    limit = options.pop("vmem", 32)
    return pl.pallas_call(
        kernel,
        out_shape=out_shape,
        name=name,
        compiler_params=pltpu.CompilerParams(vmem_limit_bytes=limit * 2**20),
        **options,
    )


def weight_kernel(*refs):
    pieces, in_ref, rest_ref, gathered_ref = refs[:4], refs[4], refs[5], refs[6]
    here = lax.axis_index("y")
    for shift, piece in zip(SHIFTS, pieces):
        start = pl.multiple_of(((here + 4 - shift) & 3) * 128, 128)
        gathered_ref[pl.ds(start, 128), :] = piece[...]

    def picked(rows, source):
        return (iota((rows, 512), 1) == source).astype(F32).astype(BF)

    row = iota((256, 512), 0)
    in_ref[...] = dot(picked(256, ((row >> 2) << 3) + (row & 3)), gathered_ref[...]).astype(BF)
    row = iota((128, 512), 0)
    base = (row >> 1) << 3
    even = (row & 1) == 0
    upper = row < 64
    wanted = (
        (jnp.where(even, base + 4, -1), jnp.where(even, -1, base + 5)),
        (jnp.where(even, -1, base + 6), jnp.where(even, base + 4, -1)),
        (jnp.where(even, base + 5, -1), jnp.where(even, -1, base + 6)),
        (jnp.where(upper, (row << 3) + 7, -1), jnp.where(upper, -1, ((row - 64) << 3) + 7)),
    )
    left = gathered_ref[:, :512]
    right = gathered_ref[:, 512:]
    for place, (from_left, from_right) in enumerate(wanted):
        new = dot(picked(128, from_left), left) + dot(picked(128, from_right), right)
        rest_ref[:, place * 512 : (place + 1) * 512] = new.astype(BF)


def seq_index():
    return lax.axis_index("x") * 2 + lax.axis_index("core")


def pack_kernel(*refs):
    ins, outs = refs[:4], refs[4:]
    here = seq_index()
    for shift, out_ref in enumerate(outs):
        start = pl.multiple_of(((here + shift) & 7) * COLS, COLS)
        for place, ref in enumerate(ins):
            out_ref[:, place * COLS : (place + 1) * COLS] = ref[:, pl.ds(start, COLS)]


def unpack_kernel(packed_ref, first_ref, second_ref, third_ref):
    for part in range(SEQ):
        for place, ref in enumerate((first_ref, second_ref, third_ref)):
            ref[:, part * COLS : (part + 1) * COLS] = packed_ref[
                part, :, place * COLS : (place + 1) * COLS
            ]


def head_weights(packed_ref, head):
    base = head * HEAD
    query = packed_ref[:, base : base + HEAD]
    key = packed_ref[:, COLS + base : COLS + base + HEAD]
    value = packed_ref[:, 2 * COLS + base : 2 * COLS + base + HEAD]
    scores = dot_nt(query, key) * HEAD ** (-0.5)
    allowed = iota((LENGTH, LENGTH), 1) <= iota((LENGTH, LENGTH), 0)
    scores = jnp.where(allowed, scores, -1e30)
    raised = jnp.exp(scores - jnp.max(scores, axis=1, keepdims=True))
    weights = raised * (1.0 / jnp.sum(raised, axis=1, keepdims=True))
    return query, key, value, weights


def forward_kernel(*refs):
    pieces, packed_ref, context_ref = refs[:SEQ], refs[SEQ], refs[SEQ + 1]
    here = seq_index()
    for shift, piece in enumerate(pieces):
        start = pl.multiple_of(((here + SEQ - shift) & 7) * FRAMES, FRAMES)
        packed_ref[pl.ds(start, FRAMES), :] = piece[...]
    for head in range(2):
        unused_q, unused_k, value, weights = head_weights(packed_ref, head)
        context_ref[:, head * HEAD : (head + 1) * HEAD] = dot(weights.astype(BF), value).astype(BF)


def enter_kernel(context_ref, w_in_ref, out_ref):
    out_ref[...] = dot(context_ref[...], w_in_ref[...]).astype(BF)


def backward_kernel(packed_ref, own_ref, near_ref, out_ref, grad_s):
    core = lax.axis_index("core")
    for x in range(4):
        for side, ref in ((core, own_ref), (1 - core, near_ref)):
            start = pl.multiple_of((2 * x + side) * FRAMES, FRAMES)
            carried = ref[x * FRAMES : (x + 1) * FRAMES, :].astype(F32)
            text = packed_ref[pl.ds(start, FRAMES), 3 * COLS :].astype(F32)
            grad_s[pl.ds(start, FRAMES), :] = (text + carried).astype(BF)
    for head in range(2):
        base = head * HEAD
        query, key, value, weights = head_weights(packed_ref, head)
        grad = grad_s[:, base : base + HEAD]
        weight_grad = dot_nt(grad, value).astype(BF).astype(F32)
        inner = jnp.sum(weight_grad * weights, axis=1, keepdims=True)
        score_grad = (weights * (weight_grad - inner) * HEAD ** (-0.5)).astype(BF)
        out_ref[:, base : base + HEAD] = dot(score_grad, key).astype(BF)
        out_ref[:, COLS + base : COLS + base + HEAD] = dot_tn(score_grad, query).astype(BF)
        out_ref[:, 2 * COLS + base : 2 * COLS + base + HEAD] = dot_tn(
            weights.astype(BF), grad
        ).astype(BF)


def routing(target_ref, active_ref):
    down = iota((FRAMES, FRAMES), 0)
    across = iota((FRAMES, FRAMES), 1)
    target_row = target_ref[...].astype(F32)
    live_row = (active_ref[...] == 1).astype(F32)
    target_col = jnp.sum(jnp.where(down == across, target_row, 0.0), axis=1, keepdims=True)
    live_col = jnp.sum(jnp.where(down == across, live_row, 0.0), axis=1, keepdims=True)
    same = target_col == target_row
    earlier_row = jnp.sum(jnp.where(same & (down < across), live_col, 0.0), axis=0, keepdims=True)
    earlier_col = jnp.sum(jnp.where(same & (across < down), live_row, 0.0), axis=1, keepdims=True)
    return (target_row, live_row, earlier_row), (target_col, live_col, earlier_col)


def narrow_to_wide(narrow_ref, scratch):
    scratch[...] = narrow_ref[...].astype(F32)
    return jnp.concatenate([scratch[pl.ds(c, SLOTS, stride=8), :] for c in range(8)], axis=1)


def wide_to_narrow(wide, narrow_ref, scratch):
    for c in range(8):
        scratch[pl.ds(c, SLOTS, stride=8), :] = wide[:, c * 128 : (c + 1) * 128]
    narrow_ref[...] = scratch[...].astype(BF)


def send_kernel(parts_ref, target_ref, active_ref, out_ref, narrow_s):
    rows = parts_ref[0].astype(F32)
    for part in range(1, SEQ):
        rows = rows + parts_ref[part].astype(F32)
    (target, live, earlier), unused = routing(target_ref, active_ref)
    slot = iota((SLOTS, FRAMES), 0)
    chosen = (
        (target == (slot >> 1).astype(F32)) & (live > 0.5) & (earlier == (slot & 1).astype(F32))
    ).astype(F32)
    sent = dot(chosen.astype(BF), rows.astype(BF))
    filled = jnp.sum(chosen, axis=1, keepdims=True) > 0.5
    wide_to_narrow(jnp.where(filled, sent, EMPTY), out_ref, narrow_s)


def parts_held():
    x, core = lax.axis_index("x"), lax.axis_index("core")
    return [((x + 4 - shift) & 3) * 2 + side for side in (core, 1 - core) for shift in SHIFTS]


def return_kernel(returned_ref, target_ref, active_ref, out_ref, narrow_s):
    unused, (target, live, earlier) = routing(target_ref, active_ref)
    slot = iota((FRAMES, SLOTS), 1)
    chosen = (
        (target == (slot >> 1).astype(F32)) & (live > 0.5) & (earlier == (slot & 1).astype(F32))
    ).astype(F32)
    returned = narrow_to_wide(returned_ref, narrow_s).astype(BF)
    rows = dot(chosen.astype(BF), returned).astype(BF)
    for x in range(4):
        out_ref[x] = rows


def carry_kernel(rows_ref, own_in_ref, near_in_ref, own_ref, near_ref):
    own_ref[...] = dot_nt(rows_ref[...], own_in_ref[...]).astype(BF)
    near_ref[...] = dot_nt(rows_ref[...], near_in_ref[...]).astype(BF)


def depth_kernel(slots_ref, codes_ref, cot_ref, gain_ref, *refs):
    pieces, refs = refs[:SEQ], refs[SEQ:]
    (
        out_ref,
        weights_s,
        hidden_s,
        cot_s,
        mixed_s,
        projected_s,
        grads_s,
        narrow_s,
        codes_s,
        given_s,
        sems,
    ) = refs
    copies = [
        pltpu.make_async_copy(codes_ref, codes_s, sems.at[0]),
        pltpu.make_async_copy(cot_ref, given_s, sems.at[1]),
    ]
    for part, piece in zip(parts_held(), pieces):
        goal = weights_s.at[pl.ds(pl.multiple_of(part * 128, 128), 128), :]
        copies.append(pltpu.make_async_copy(piece, goal, sems.at[len(copies)]))
    for copy in copies:
        copy.start()

    slots = narrow_to_wide(slots_ref, narrow_s).astype(BF)
    live_col = (slots[:, 0:1].astype(F32) < EMPTY * 0.5).astype(F32)
    down = iota((SLOTS, SLOTS), 0)
    across = iota((SLOTS, SLOTS), 1)
    live_row = jnp.sum(jnp.where(down == across, live_col, 0.0), axis=0, keepdims=True)
    rank_row = jnp.sum(jnp.where(down < across, live_col, 0.0), axis=0, keepdims=True)
    rank_col = jnp.sum(jnp.where(across < down, live_row, 0.0), axis=1, keepdims=True)

    spread = (
        (live_row > 0.5) & (rank_row == (iota((PADDED, SLOTS), 0) >> 3).astype(F32))
    ).astype(F32)
    spare = jnp.zeros((PADDED - ROWS, D_DEP), F32)
    copies[0].wait()
    hidden = dot(spread.astype(BF), slots) + jnp.concatenate(
        [codes_s[...].astype(F32), spare], axis=0
    )
    hidden_s[...] = hidden
    copies[1].wait()
    cot_s[...] = jnp.concatenate([given_s[...].astype(F32), spare], axis=0)
    gain = gain_ref[...].astype(F32)
    scale = lax.rsqrt(jnp.sum(hidden * hidden, axis=1, keepdims=True) * (1.0 / D_DEP) + 1e-05)
    normed = (hidden * scale * gain).astype(BF)
    for copy in copies[2:]:
        copy.wait()
    width = DHEADS * DHEAD
    w_out = weights_s[:, 3 * width :].reshape(SEQ, 2, DHEAD, width)
    mixed_grad = dot_nt(cot_s[:, :width].astype(BF), w_out[:, 0].reshape(width, width))
    mixed_grad += dot_nt(cot_s[:, width:].astype(BF), w_out[:, 1].reshape(width, width))
    mixed_s[...] = mixed_grad.astype(BF)
    projected_s[...] = dot(normed, weights_s[:, : 3 * width]).astype(BF)

    first_half = iota((GROUP, 128), 1) < DHEAD
    nothing = jnp.zeros((GROUP, 128), BF)
    frame = iota((GROUP // CODES, CODES, 2 * GROUP), 0)
    row = iota((GROUP // CODES, CODES, 2 * GROUP), 2) & (GROUP - 1)
    same_frame = frame == (row >> 3)

    def halves(array):
        return jnp.concatenate(
            [jnp.where(first_half, array, nothing), jnp.where(first_half, nothing, array)], axis=0
        )

    def own_frame(array):
        blocks = array.reshape(GROUP // CODES, CODES, 2 * GROUP)
        return jnp.sum(jnp.where(same_frame, blocks, 0.0), axis=0)

    def all_frames(array):
        blocks = jnp.where(same_frame, array[None], 0.0)
        return blocks.reshape(GROUP, 2 * GROUP).astype(BF)

    units = [
        (slice(group * GROUP, (group + 1) * GROUP), pair * 128)
        for group in range(PADDED // GROUP)
        for pair in range(DHEADS // 2)
    ]
    scores, weight_grad = [], []
    for rows, lanes in units:
        key = projected_s[rows, width + lanes : width + lanes + 128]
        value = projected_s[rows, 2 * width + lanes : 2 * width + lanes + 128]
        scores.append(own_frame(dot_nt(key, halves(projected_s[rows, lanes : lanes + 128]))))
        weight_grad.append(own_frame(dot_nt(value, halves(mixed_s[rows, lanes : lanes + 128]))))
    scores = jnp.concatenate(scores, axis=1) * DHEAD ** (-0.5)
    scores = jnp.where((iota(scores.shape, 0) <= (iota(scores.shape, 1) & 7)), scores, -1e30)
    raised = jnp.exp(scores - jnp.max(scores, axis=0, keepdims=True))
    weights = raised * (1.0 / jnp.sum(raised, axis=0, keepdims=True))
    weight_grad = jnp.concatenate(weight_grad, axis=1).astype(BF).astype(F32)
    inner = jnp.sum(weight_grad * weights, axis=0, keepdims=True)
    score_grad = weights * (weight_grad - inner) * DHEAD ** (-0.5)
    for place, (rows, lanes) in enumerate(units):
        own = slice(place * 2 * GROUP, (place + 1) * 2 * GROUP)
        back = all_frames(score_grad[:, own])
        query_grad = dot_tn(back, projected_s[rows, width + lanes : width + lanes + 128])
        grads_s[rows, lanes : lanes + 128] = jnp.where(
            first_half, query_grad[:GROUP], query_grad[GROUP:]
        ).astype(BF)
        grads_s[rows, width + lanes : width + lanes + 128] = dot(
            back, halves(projected_s[rows, lanes : lanes + 128])
        ).astype(BF)
        grads_s[rows, 2 * width + lanes : 2 * width + lanes + 128] = dot(
            all_frames(weights[:, own]), halves(mixed_s[rows, lanes : lanes + 128])
        ).astype(BF)
    normed_grad = dot_nt(grads_s[...], weights_s[:, : 3 * width]).astype(BF).astype(F32) * gain
    hidden = hidden_s[...]
    inner = jnp.sum(normed_grad * hidden, axis=1, keepdims=True) * (1.0 / D_DEP)
    hidden_grad = cot_s[...] + scale * normed_grad - hidden * (scale * scale * scale * inner)
    frames = jnp.sum(hidden_grad.reshape(FRAMES, CODES, D_DEP), axis=1)

    back = ((live_col > 0.5) & (rank_col == iota((SLOTS, FRAMES), 1).astype(F32))).astype(F32)
    wide_to_narrow(dot(back.astype(BF), frames.astype(BF)), out_ref, narrow_s)


def depth_scratch():
    width = DHEADS * DHEAD
    return [
        pltpu.VMEM((D_DEP, 4 * width), BF),
        pltpu.VMEM((PADDED, D_DEP), F32),
        pltpu.VMEM((PADDED, D_DEP), F32),
        pltpu.VMEM((PADDED, width), BF),
        pltpu.VMEM((PADDED, 3 * width), BF),
        pltpu.VMEM((PADDED, 3 * width), BF),
        pltpu.VMEM((SLOTS * 8, 128), F32),
        pltpu.VMEM((ROWS, D_DEP), BF),
        pltpu.VMEM((ROWS, D_DEP), BF),
        pltpu.SemaphoreType.DMA((SEQ + 2,)),
    ]


def exchange(array, axis):
    return lax.all_to_all(array, axis, split_axis=0, concat_axis=0, tiled=True)


def moved(array, axis, size, shift):
    return lax.ppermute(array, axis, [(i, (i + shift) % size) for i in range(size)])


def shards(
    queries,
    keys,
    values,
    text_grad,
    active,
    target,
    codes,
    depth_cot,
    w_in,
    norm_gain,
    w_qkv,
    w_out,
):
    seq = ("x", "core")
    owner = ("y", "z")
    mine = jnp.concatenate([w_in, w_qkv, w_out]).reshape(1, 8, D_DEP)
    along_z = exchange(jnp.broadcast_to(mine, (16, 8, D_DEP)), "z").reshape(128, D_DEP)
    along_y = [along_z] + [moved(along_z, "y", 4, shift) for shift in SHIFTS[1:]]
    own_in, own_rest = call(
        weight_kernel,
        (jax.ShapeDtypeStruct((256, D_DEP), BF), jax.ShapeDtypeStruct((128, 2 * D_DEP), BF)),
        "sort_weights",
        scratch_shapes=[pltpu.VMEM((512, D_DEP), BF)],
    )(*along_y)
    rest = [own_rest] + [moved(own_rest, "x", 4, shift) for shift in SHIFTS[1:]]
    rest += [moved(piece, "core", 2, 1) for piece in rest]

    block = jax.ShapeDtypeStruct((FRAMES, 4 * COLS), BF)
    blocks = call(pack_kernel, [block] * SEQ, "pack_heads")(
        queries[0], keys[0], values[0], text_grad[0]
    )
    blocks = [blocks[0]] + [moved(blocks[k], seq, SEQ, k) for k in range(1, SEQ)]
    packed, context = call(
        forward_kernel,
        (
            jax.ShapeDtypeStruct((LENGTH, 4 * COLS), BF),
            jax.ShapeDtypeStruct((LENGTH, COLS), BF),
        ),
        "attention_forward",
    )(*blocks)
    parts = call(enter_kernel, jax.ShapeDtypeStruct((LENGTH, D_DEP), BF), "enter_depth")(
        context, own_in
    )
    parts = exchange(parts.reshape(SEQ, FRAMES, D_DEP), seq)
    narrow = jax.ShapeDtypeStruct((SLOTS * 8, 128), BF)
    sent = call(
        send_kernel, narrow, "send_rows", scratch_shapes=[pltpu.VMEM((SLOTS * 8, 128), F32)]
    )(parts, target, active)
    slots = exchange(sent.reshape(OWNERS, 16, 128), owner).reshape(SLOTS * 8, 128)
    vmem = pl.BlockSpec(memory_space=pltpu.VMEM)
    anywhere = pl.BlockSpec(memory_space=pl.ANY)
    grads = call(
        depth_kernel,
        narrow,
        "depth_layer",
        in_specs=[vmem, anywhere, anywhere, vmem] + [anywhere] * SEQ,
        out_specs=vmem,
        scratch_shapes=depth_scratch(),
        vmem=58,
    )(
        slots,
        codes.reshape(ROWS, D_DEP),
        depth_cot.reshape(ROWS, D_DEP),
        norm_gain.reshape(1, D_DEP),
        *rest,
    )
    late_in, unused = lax.optimization_barrier((own_in, grads))
    near_in = moved(late_in, "core", 2, 1)
    returned = exchange(grads.reshape(OWNERS, 16, 128), owner).reshape(SLOTS * 8, 128)
    rows = call(
        return_kernel,
        jax.ShapeDtypeStruct((4, FRAMES, D_DEP), BF),
        "return_rows",
        scratch_shapes=[pltpu.VMEM((SLOTS * 8, 128), F32)],
    )(returned, target, active)
    rows = exchange(rows, "x").reshape(4 * FRAMES, D_DEP)
    half = jax.ShapeDtypeStruct((4 * FRAMES, COLS), BF)
    own_carried, near_carried = call(carry_kernel, (half, half), "context_grads")(
        rows, own_in, near_in
    )
    grads = call(
        backward_kernel,
        jax.ShapeDtypeStruct((LENGTH, 3 * COLS), BF),
        "attention_backward",
        scratch_shapes=[pltpu.VMEM((LENGTH, COLS), BF)],
    )(packed, own_carried, moved(near_carried, "core", 2, 1))
    grads = exchange(grads.reshape(SEQ, FRAMES, 3 * COLS), seq)
    shape = jax.ShapeDtypeStruct((FRAMES, D_CTX), BF)
    query_grad, key_grad, value_grad = call(unpack_kernel, (shape, shape, shape), "unpack_grads")(grads)
    return query_grad[None], key_grad[None], value_grad[None]


def solution(mesh):
    split = Mesh(mesh.devices.reshape(4, 2, 4, 16), ("x", "core", "y", "z"))
    rows = P(("y", "z"), ("x", "core"), None)
    frames = P(("y", "z"), ("x", "core"))
    code_rows = P(("y", "z"), ("x", "core"), None, None)
    flat = P(("x", "core", "y", "z"))
    in_specs = (
        rows,
        rows,
        rows,
        rows,
        frames,
        frames,
        code_rows,
        code_rows,
        flat,
        P(),
        flat,
        flat,
    )
    return jax.shard_map(
        shards, mesh=split, in_specs=in_specs, out_specs=(rows, rows, rows), check_vma=False
    )
```

```python
import jax
import jax.numpy as jnp
from jax import lax
from jax.experimental import pallas as pl
from jax.experimental.pallas import tpu as pltpu
from jax.sharding import Mesh
from jax.sharding import PartitionSpec as P

HEADS = 16
HEAD = 128
D_DEP = 1024
DHEADS = 8
DHEAD = 64
CODES = 8
D_CTX = 2048
FRAMES = 64
SEQ = 8
OWNERS = 64
CAP = 2
SLOTS = OWNERS * CAP
RECEIVED = 59
LENGTH = SEQ * FRAMES
COLS = D_CTX // SEQ
ROWS = RECEIVED * CODES
PADDED = 512
GROUP = 128
EMPTY = 2.0**100
SHIFTS = (0, 1, 3, 2)
BF = jnp.bfloat16
F32 = jnp.float32


def dot(a, b):
    return jnp.dot(a, b, preferred_element_type=F32)


def dot_nt(a, b):
    return lax.dot_general(a, b, (((1,), (1,)), ((), ())), preferred_element_type=F32)


def dot_tn(a, b):
    return lax.dot_general(a, b, (((0,), (0,)), ((), ())), preferred_element_type=F32)


def iota(shape, axis):
    return lax.broadcasted_iota(jnp.int32, shape, axis)


def call(kernel, out_shape, name, **options):
    limit = options.pop("vmem", 32)
    return pl.pallas_call(
        kernel,
        out_shape=out_shape,
        name=name,
        compiler_params=pltpu.CompilerParams(vmem_limit_bytes=limit * 2**20),
        **options,
    )


def enter_kernel(*refs):
    pieces, (context_ref, in_ref, rest_ref, out_ref, gathered_ref) = refs[:4], refs[4:]
    here = lax.axis_index("y")
    for shift, piece in zip(SHIFTS, pieces):
        start = pl.multiple_of(((here + 4 - shift) & 3) * 128, 128)
        gathered_ref[pl.ds(start, 128), :] = piece[...]

    def picked(rows, source):
        return (iota((rows, 512), 1) == source).astype(F32).astype(BF)

    row = iota((256, 512), 0)
    w_in = dot(picked(256, ((row >> 2) << 3) + (row & 3)), gathered_ref[...]).astype(BF)
    in_ref[...] = w_in
    out_ref[...] = dot(context_ref[...], w_in).astype(BF)
    row = iota((128, 512), 0)
    base = (row >> 1) << 3
    even = (row & 1) == 0
    upper = row < 64
    wanted = (
        (jnp.where(even, base + 4, -1), jnp.where(even, -1, base + 5)),
        (jnp.where(even, -1, base + 6), jnp.where(even, base + 4, -1)),
        (jnp.where(even, base + 5, -1), jnp.where(even, -1, base + 6)),
        (jnp.where(upper, (row << 3) + 7, -1), jnp.where(upper, -1, ((row - 64) << 3) + 7)),
    )
    left = gathered_ref[:, :512]
    right = gathered_ref[:, 512:]
    for place, (from_left, from_right) in enumerate(wanted):
        new = dot(picked(128, from_left), left) + dot(picked(128, from_right), right)
        rest_ref[:, place * 512 : (place + 1) * 512] = new.astype(BF)


def seq_index():
    return lax.axis_index("x") * 2 + lax.axis_index("core")


def pack_kernel(*refs):
    ins, outs = refs[:4], refs[4:]
    here = seq_index()
    for shift, out_ref in enumerate(outs):
        start = pl.multiple_of(((here + shift) & 7) * COLS, COLS)
        for place, ref in enumerate(ins):
            out_ref[:, place * COLS : (place + 1) * COLS] = ref[:, pl.ds(start, COLS)]


def unpack_kernel(packed_ref, first_ref, second_ref, third_ref):
    for part in range(SEQ):
        for place, ref in enumerate((first_ref, second_ref, third_ref)):
            ref[:, part * COLS : (part + 1) * COLS] = packed_ref[
                part, :, place * COLS : (place + 1) * COLS
            ]


def head_weights(packed_ref, head):
    base = head * HEAD
    query = packed_ref[:, base : base + HEAD]
    key = packed_ref[:, COLS + base : COLS + base + HEAD]
    value = packed_ref[:, 2 * COLS + base : 2 * COLS + base + HEAD]
    scores = dot_nt(query, key) * HEAD ** (-0.5)
    allowed = iota((LENGTH, LENGTH), 1) <= iota((LENGTH, LENGTH), 0)
    scores = jnp.where(allowed, scores, -1e30)
    raised = jnp.exp(scores - jnp.max(scores, axis=1, keepdims=True))
    weights = raised * (1.0 / jnp.sum(raised, axis=1, keepdims=True))
    return query, key, value, weights


def forward_kernel(*refs):
    pieces, packed_ref, context_ref = refs[:SEQ], refs[SEQ], refs[SEQ + 1]
    here = seq_index()
    for shift, piece in enumerate(pieces):
        start = pl.multiple_of(((here + SEQ - shift) & 7) * FRAMES, FRAMES)
        packed_ref[pl.ds(start, FRAMES), :] = piece[...]
    for head in range(2):
        unused_q, unused_k, value, weights = head_weights(packed_ref, head)
        context_ref[:, head * HEAD : (head + 1) * HEAD] = dot(weights.astype(BF), value).astype(BF)


def backward_kernel(packed_ref, own_ref, near_ref, out_ref, grad_s):
    core = lax.axis_index("core")
    for x in range(4):
        for side, ref in ((core, own_ref), (1 - core, near_ref)):
            start = pl.multiple_of((2 * x + side) * FRAMES, FRAMES)
            carried = ref[x * FRAMES : (x + 1) * FRAMES, :].astype(F32)
            text = packed_ref[pl.ds(start, FRAMES), 3 * COLS :].astype(F32)
            grad_s[pl.ds(start, FRAMES), :] = (text + carried).astype(BF)
    for head in range(2):
        base = head * HEAD
        query, key, value, weights = head_weights(packed_ref, head)
        grad = grad_s[:, base : base + HEAD]
        weight_grad = dot_nt(grad, value).astype(BF).astype(F32)
        inner = jnp.sum(weight_grad * weights, axis=1, keepdims=True)
        score_grad = (weights * (weight_grad - inner) * HEAD ** (-0.5)).astype(BF)
        out_ref[:, base : base + HEAD] = dot(score_grad, key).astype(BF)
        out_ref[:, COLS + base : COLS + base + HEAD] = dot_tn(score_grad, query).astype(BF)
        out_ref[:, 2 * COLS + base : 2 * COLS + base + HEAD] = dot_tn(
            weights.astype(BF), grad
        ).astype(BF)


def routing(target_ref, active_ref):
    down = iota((FRAMES, FRAMES), 0)
    across = iota((FRAMES, FRAMES), 1)
    target_row = target_ref[...].astype(F32)
    live_row = (active_ref[...] == 1).astype(F32)
    target_col = jnp.sum(jnp.where(down == across, target_row, 0.0), axis=1, keepdims=True)
    live_col = jnp.sum(jnp.where(down == across, live_row, 0.0), axis=1, keepdims=True)
    same = target_col == target_row
    earlier_row = jnp.sum(jnp.where(same & (down < across), live_col, 0.0), axis=0, keepdims=True)
    earlier_col = jnp.sum(jnp.where(same & (across < down), live_row, 0.0), axis=1, keepdims=True)
    return (target_row, live_row, earlier_row), (target_col, live_col, earlier_col)


def narrow_to_wide(narrow_ref, scratch):
    scratch[...] = narrow_ref[...].astype(F32)
    return jnp.concatenate([scratch[pl.ds(c, SLOTS, stride=8), :] for c in range(8)], axis=1)


def wide_to_narrow(wide, narrow_ref, scratch):
    for c in range(8):
        scratch[pl.ds(c, SLOTS, stride=8), :] = wide[:, c * 128 : (c + 1) * 128]
    narrow_ref[...] = scratch[...].astype(BF)


def send_kernel(parts_ref, target_ref, active_ref, out_ref, narrow_s):
    rows = parts_ref[0].astype(F32)
    for part in range(1, SEQ):
        rows = rows + parts_ref[part].astype(F32)
    (target, live, earlier), unused = routing(target_ref, active_ref)
    slot = iota((SLOTS, FRAMES), 0)
    chosen = (
        (target == (slot >> 1).astype(F32)) & (live > 0.5) & (earlier == (slot & 1).astype(F32))
    ).astype(F32)
    sent = dot(chosen.astype(BF), rows.astype(BF))
    filled = jnp.sum(chosen, axis=1, keepdims=True) > 0.5
    wide_to_narrow(jnp.where(filled, sent, EMPTY), out_ref, narrow_s)


def parts_held():
    x, core = lax.axis_index("x"), lax.axis_index("core")
    return [((x + 4 - shift) & 3) * 2 + side for side in (core, 1 - core) for shift in SHIFTS]


def return_kernel(returned_ref, target_ref, active_ref, out_ref, narrow_s):
    unused, (target, live, earlier) = routing(target_ref, active_ref)
    slot = iota((FRAMES, SLOTS), 1)
    chosen = (
        (target == (slot >> 1).astype(F32)) & (live > 0.5) & (earlier == (slot & 1).astype(F32))
    ).astype(F32)
    returned = narrow_to_wide(returned_ref, narrow_s).astype(BF)
    rows = dot(chosen.astype(BF), returned).astype(BF)
    for x in range(4):
        out_ref[x] = rows


def carry_kernel(rows_ref, own_in_ref, near_in_ref, own_ref, near_ref):
    own_ref[...] = dot_nt(rows_ref[...], own_in_ref[...]).astype(BF)
    near_ref[...] = dot_nt(rows_ref[...], near_in_ref[...]).astype(BF)


def depth_kernel(slots_ref, codes_ref, cot_ref, gain_ref, *refs):
    pieces, refs = refs[:SEQ], refs[SEQ:]
    (
        out_ref,
        weights_s,
        hidden_s,
        cot_s,
        mixed_s,
        projected_s,
        grads_s,
        narrow_s,
        codes_s,
        given_s,
        sems,
    ) = refs
    copies = [
        pltpu.make_async_copy(codes_ref, codes_s, sems.at[0]),
        pltpu.make_async_copy(cot_ref, given_s, sems.at[1]),
    ]
    for part, piece in zip(parts_held(), pieces):
        goal = weights_s.at[pl.ds(pl.multiple_of(part * 128, 128), 128), :]
        copies.append(pltpu.make_async_copy(piece, goal, sems.at[len(copies)]))
    for copy in copies:
        copy.start()

    slots = narrow_to_wide(slots_ref, narrow_s).astype(BF)
    live_col = (slots[:, 0:1].astype(F32) < EMPTY * 0.5).astype(F32)
    down = iota((SLOTS, SLOTS), 0)
    across = iota((SLOTS, SLOTS), 1)
    live_row = jnp.sum(jnp.where(down == across, live_col, 0.0), axis=0, keepdims=True)
    rank_row = jnp.sum(jnp.where(down < across, live_col, 0.0), axis=0, keepdims=True)
    rank_col = jnp.sum(jnp.where(across < down, live_row, 0.0), axis=1, keepdims=True)

    spread = (
        (live_row > 0.5) & (rank_row == (iota((PADDED, SLOTS), 0) >> 3).astype(F32))
    ).astype(F32)
    spare = jnp.zeros((PADDED - ROWS, D_DEP), F32)
    copies[0].wait()
    hidden = dot(spread.astype(BF), slots) + jnp.concatenate(
        [codes_s[...].astype(F32), spare], axis=0
    )
    hidden_s[...] = hidden
    copies[1].wait()
    cot_s[...] = jnp.concatenate([given_s[...].astype(F32), spare], axis=0)
    gain = jnp.concatenate([gain_ref[c : c + 1, :].astype(F32) for c in range(8)], axis=1)
    scale = lax.rsqrt(jnp.sum(hidden * hidden, axis=1, keepdims=True) * (1.0 / D_DEP) + 1e-05)
    normed = (hidden * scale * gain).astype(BF)
    for copy in copies[2:]:
        copy.wait()
    width = DHEADS * DHEAD
    w_out = weights_s[:, 3 * width :].reshape(SEQ, 2, DHEAD, width)
    mixed_grad = dot_nt(cot_s[:, :width].astype(BF), w_out[:, 0].reshape(width, width))
    mixed_grad += dot_nt(cot_s[:, width:].astype(BF), w_out[:, 1].reshape(width, width))
    mixed_s[...] = mixed_grad.astype(BF)
    projected_s[...] = dot(normed, weights_s[:, : 3 * width]).astype(BF)

    first_half = iota((GROUP, 128), 1) < DHEAD
    nothing = jnp.zeros((GROUP, 128), BF)
    frame = iota((GROUP // CODES, CODES, 2 * GROUP), 0)
    row = iota((GROUP // CODES, CODES, 2 * GROUP), 2) & (GROUP - 1)
    same_frame = frame == (row >> 3)

    def halves(array):
        return jnp.concatenate(
            [jnp.where(first_half, array, nothing), jnp.where(first_half, nothing, array)], axis=0
        )

    def own_frame(array):
        blocks = array.reshape(GROUP // CODES, CODES, 2 * GROUP)
        return jnp.sum(jnp.where(same_frame, blocks, 0.0), axis=0)

    def all_frames(array):
        blocks = jnp.where(same_frame, array[None], 0.0)
        return blocks.reshape(GROUP, 2 * GROUP).astype(BF)

    units = [
        (slice(group * GROUP, (group + 1) * GROUP), pair * 128)
        for group in range(PADDED // GROUP)
        for pair in range(DHEADS // 2)
    ]
    scores, weight_grad = [], []
    for rows, lanes in units:
        key = projected_s[rows, width + lanes : width + lanes + 128]
        value = projected_s[rows, 2 * width + lanes : 2 * width + lanes + 128]
        scores.append(own_frame(dot_nt(key, halves(projected_s[rows, lanes : lanes + 128]))))
        weight_grad.append(own_frame(dot_nt(value, halves(mixed_s[rows, lanes : lanes + 128]))))
    scores = jnp.concatenate(scores, axis=1) * DHEAD ** (-0.5)
    scores = jnp.where((iota(scores.shape, 0) <= (iota(scores.shape, 1) & 7)), scores, -1e30)
    raised = jnp.exp(scores - jnp.max(scores, axis=0, keepdims=True))
    weights = raised * (1.0 / jnp.sum(raised, axis=0, keepdims=True))
    weight_grad = jnp.concatenate(weight_grad, axis=1).astype(BF).astype(F32)
    inner = jnp.sum(weight_grad * weights, axis=0, keepdims=True)
    score_grad = weights * (weight_grad - inner) * DHEAD ** (-0.5)
    for place, (rows, lanes) in enumerate(units):
        own = slice(place * 2 * GROUP, (place + 1) * 2 * GROUP)
        back = all_frames(score_grad[:, own])
        query_grad = dot_tn(back, projected_s[rows, width + lanes : width + lanes + 128])
        grads_s[rows, lanes : lanes + 128] = jnp.where(
            first_half, query_grad[:GROUP], query_grad[GROUP:]
        ).astype(BF)
        grads_s[rows, width + lanes : width + lanes + 128] = dot(
            back, halves(projected_s[rows, lanes : lanes + 128])
        ).astype(BF)
        grads_s[rows, 2 * width + lanes : 2 * width + lanes + 128] = dot(
            all_frames(weights[:, own]), halves(mixed_s[rows, lanes : lanes + 128])
        ).astype(BF)
    normed_grad = dot_nt(grads_s[...], weights_s[:, : 3 * width]).astype(BF).astype(F32) * gain
    hidden = hidden_s[...]
    inner = jnp.sum(normed_grad * hidden, axis=1, keepdims=True) * (1.0 / D_DEP)
    hidden_grad = cot_s[...] + scale * normed_grad - hidden * (scale * scale * scale * inner)
    frames = jnp.sum(hidden_grad.reshape(FRAMES, CODES, D_DEP), axis=1)

    back = ((live_col > 0.5) & (rank_col == iota((SLOTS, FRAMES), 1).astype(F32))).astype(F32)
    wide_to_narrow(dot(back.astype(BF), frames.astype(BF)), out_ref, narrow_s)


def depth_scratch():
    width = DHEADS * DHEAD
    return [
        pltpu.VMEM((D_DEP, 4 * width), BF),
        pltpu.VMEM((PADDED, D_DEP), F32),
        pltpu.VMEM((PADDED, D_DEP), F32),
        pltpu.VMEM((PADDED, width), BF),
        pltpu.VMEM((PADDED, 3 * width), BF),
        pltpu.VMEM((PADDED, 3 * width), BF),
        pltpu.VMEM((SLOTS * 8, 128), F32),
        pltpu.VMEM((ROWS, D_DEP), BF),
        pltpu.VMEM((ROWS, D_DEP), BF),
        pltpu.SemaphoreType.DMA((SEQ + 2,)),
    ]


def exchange(array, axis):
    return lax.all_to_all(array, axis, split_axis=0, concat_axis=0, tiled=True)


def moved(array, axis, size, shift):
    return lax.ppermute(array, axis, [(i, (i + shift) % size) for i in range(size)])


def shards(
    queries,
    keys,
    values,
    text_grad,
    active,
    target,
    codes,
    depth_cot,
    w_in,
    norm_gain,
    w_qkv,
    w_out,
):
    seq = ("x", "core")
    owner = ("y", "z")
    mine = jnp.concatenate([w_in, w_qkv, w_out]).reshape(1, 8, D_DEP)
    along_z = exchange(jnp.broadcast_to(mine, (16, 8, D_DEP)), "z").reshape(128, D_DEP)
    along_y = [along_z] + [moved(along_z, "y", 4, shift) for shift in SHIFTS[1:]]
    block = jax.ShapeDtypeStruct((FRAMES, 4 * COLS), BF)
    blocks = call(pack_kernel, [block] * SEQ, "pack_heads")(
        queries[0], keys[0], values[0], text_grad[0]
    )
    blocks = [blocks[0]] + [moved(blocks[k], seq, SEQ, k) for k in range(1, SEQ)]
    packed, context = call(
        forward_kernel,
        (
            jax.ShapeDtypeStruct((LENGTH, 4 * COLS), BF),
            jax.ShapeDtypeStruct((LENGTH, COLS), BF),
        ),
        "attention_forward",
    )(*blocks)
    own_in, own_rest, parts = call(
        enter_kernel,
        (
            jax.ShapeDtypeStruct((COLS, D_DEP), BF),
            jax.ShapeDtypeStruct((128, 2 * D_DEP), BF),
            jax.ShapeDtypeStruct((LENGTH, D_DEP), BF),
        ),
        "enter_depth",
        scratch_shapes=[pltpu.VMEM((512, D_DEP), BF)],
    )(*along_y, context)
    far_rest = [moved(own_rest, "x", 4, shift) for shift in SHIFTS[1:]]
    parts = exchange(parts.reshape(SEQ, FRAMES, D_DEP), seq)
    parts, near_rest = lax.optimization_barrier((parts, moved(own_rest, "core", 2, 1)))
    rest = [own_rest, *far_rest, near_rest] + [moved(piece, "core", 2, 1) for piece in far_rest]
    narrow = jax.ShapeDtypeStruct((SLOTS * 8, 128), BF)
    sent = call(
        send_kernel, narrow, "send_rows", scratch_shapes=[pltpu.VMEM((SLOTS * 8, 128), F32)]
    )(parts, target, active)
    slots = exchange(sent.reshape(OWNERS, 16, 128), owner).reshape(SLOTS * 8, 128)
    vmem = pl.BlockSpec(memory_space=pltpu.VMEM)
    anywhere = pl.BlockSpec(memory_space=pl.ANY)
    grads = call(
        depth_kernel,
        narrow,
        "depth_layer",
        in_specs=[vmem, anywhere, anywhere, vmem] + [anywhere] * SEQ,
        out_specs=vmem,
        scratch_shapes=depth_scratch(),
        vmem=58,
    )(
        slots,
        codes.reshape(ROWS, D_DEP),
        depth_cot.reshape(ROWS, D_DEP),
        norm_gain.reshape(8, 128),
        *rest,
    )
    late_in, unused = lax.optimization_barrier((own_in, grads))
    near_in = moved(late_in, "core", 2, 1)
    returned = exchange(grads.reshape(OWNERS, 16, 128), owner).reshape(SLOTS * 8, 128)
    rows = call(
        return_kernel,
        jax.ShapeDtypeStruct((4, FRAMES, D_DEP), BF),
        "return_rows",
        scratch_shapes=[pltpu.VMEM((SLOTS * 8, 128), F32)],
    )(returned, target, active)
    rows = exchange(rows, "x").reshape(4 * FRAMES, D_DEP)
    half = jax.ShapeDtypeStruct((4 * FRAMES, COLS), BF)
    own_carried, near_carried = call(carry_kernel, (half, half), "context_grads")(
        rows, own_in, near_in
    )
    grads = call(
        backward_kernel,
        jax.ShapeDtypeStruct((LENGTH, 3 * COLS), BF),
        "attention_backward",
        scratch_shapes=[pltpu.VMEM((LENGTH, COLS), BF)],
    )(packed, own_carried, moved(near_carried, "core", 2, 1))
    grads = exchange(grads.reshape(SEQ, FRAMES, 3 * COLS), seq)
    shape = jax.ShapeDtypeStruct((FRAMES, D_CTX), BF)
    query_grad, key_grad, value_grad = call(unpack_kernel, (shape, shape, shape), "unpack_grads")(grads)
    return query_grad[None], key_grad[None], value_grad[None]


def solution(mesh):
    split = Mesh(mesh.devices.reshape(4, 2, 4, 16), ("x", "core", "y", "z"))
    rows = P(("y", "z"), ("x", "core"), None)
    frames = P(("y", "z"), ("x", "core"))
    code_rows = P(("y", "z"), ("x", "core"), None, None)
    flat = P(("x", "core", "y", "z"))
    in_specs = (
        rows,
        rows,
        rows,
        rows,
        frames,
        frames,
        code_rows,
        code_rows,
        flat,
        P(),
        flat,
        flat,
    )
    return jax.shard_map(
        shards, mesh=split, in_specs=in_specs, out_specs=(rows, rows, rows), check_vma=False
    )
```

```python
import jax
import jax.numpy as jnp
from jax import lax
from jax.experimental import pallas as pl
from jax.experimental.pallas import tpu as pltpu
from jax.sharding import Mesh
from jax.sharding import PartitionSpec as P

HEADS = 16
HEAD = 128
D_DEP = 1024
DHEADS = 8
DHEAD = 64
CODES = 8
D_CTX = 2048
FRAMES = 64
SEQ = 8
OWNERS = 64
CAP = 2
SLOTS = OWNERS * CAP
RECEIVED = 59
LENGTH = SEQ * FRAMES
COLS = D_CTX // SEQ
ROWS = RECEIVED * CODES
PADDED = 512
GROUP = 128
EMPTY = 2.0**100
SHIFTS = (0, 1, 3, 2)
BF = jnp.bfloat16
F32 = jnp.float32


def dot(a, b):
    return jnp.dot(a, b, preferred_element_type=F32)


def dot_nt(a, b):
    return lax.dot_general(a, b, (((1,), (1,)), ((), ())), preferred_element_type=F32)


def dot_tn(a, b):
    return lax.dot_general(a, b, (((0,), (0,)), ((), ())), preferred_element_type=F32)


def iota(shape, axis):
    return lax.broadcasted_iota(jnp.int32, shape, axis)


def call(kernel, out_shape, name, **options):
    limit = options.pop("vmem", 32)
    return pl.pallas_call(
        kernel,
        out_shape=out_shape,
        name=name,
        compiler_params=pltpu.CompilerParams(vmem_limit_bytes=limit * 2**20),
        **options,
    )


def enter_kernel(*refs):
    pieces, (context_ref, in_ref, rest_ref, out_ref, gathered_ref) = refs[:4], refs[4:]
    here = lax.axis_index("y")
    for shift, piece in zip(SHIFTS, pieces):
        start = pl.multiple_of(((here + 4 - shift) & 3) * 128, 128)
        gathered_ref[pl.ds(start, 128), :] = piece[...]

    def picked(rows, source):
        return (iota((rows, 512), 1) == source).astype(F32).astype(BF)

    row = iota((256, 512), 0)
    w_in = dot(picked(256, ((row >> 2) << 3) + (row & 3)), gathered_ref[...]).astype(BF)
    in_ref[...] = w_in
    out_ref[...] = dot(context_ref[...], w_in).astype(BF)
    row = iota((128, 512), 0)
    base = (row >> 1) << 3
    even = (row & 1) == 0
    upper = row < 64
    wanted = (
        (jnp.where(even, base + 4, -1), jnp.where(even, -1, base + 5)),
        (jnp.where(even, -1, base + 6), jnp.where(even, base + 4, -1)),
        (jnp.where(even, base + 5, -1), jnp.where(even, -1, base + 6)),
        (jnp.where(upper, (row << 3) + 7, -1), jnp.where(upper, -1, ((row - 64) << 3) + 7)),
    )
    left = gathered_ref[:, :512]
    right = gathered_ref[:, 512:]
    for place, (from_left, from_right) in enumerate(wanted):
        new = dot(picked(128, from_left), left) + dot(picked(128, from_right), right)
        rest_ref[:, place * 512 : (place + 1) * 512] = new.astype(BF)


def seq_index():
    return lax.axis_index("x") * 2 + lax.axis_index("core")


def pack_kernel(*refs):
    ins, outs = refs[:4], refs[4:]
    here = seq_index()
    for shift, out_ref in enumerate(outs):
        start = pl.multiple_of(((here + shift) & 7) * COLS, COLS)
        for place, ref in enumerate(ins):
            out_ref[:, place * COLS : (place + 1) * COLS] = ref[:, pl.ds(start, COLS)]


def unpack_kernel(packed_ref, first_ref, second_ref, third_ref):
    for part in range(SEQ):
        for place, ref in enumerate((first_ref, second_ref, third_ref)):
            ref[:, part * COLS : (part + 1) * COLS] = packed_ref[
                part, :, place * COLS : (place + 1) * COLS
            ]


def head_weights(packed_ref, head):
    base = head * HEAD
    query = packed_ref[:, base : base + HEAD]
    key = packed_ref[:, COLS + base : COLS + base + HEAD]
    value = packed_ref[:, 2 * COLS + base : 2 * COLS + base + HEAD]
    scores = dot_nt(query, key) * HEAD ** (-0.5)
    allowed = iota((LENGTH, LENGTH), 1) <= iota((LENGTH, LENGTH), 0)
    scores = jnp.where(allowed, scores, -1e30)
    raised = jnp.exp(scores - jnp.max(scores, axis=1, keepdims=True))
    weights = raised * (1.0 / jnp.sum(raised, axis=1, keepdims=True))
    return query, key, value, weights


def forward_kernel(*refs):
    pieces, packed_ref, context_ref = refs[:SEQ], refs[SEQ], refs[SEQ + 1]
    here = seq_index()
    for shift, piece in enumerate(pieces):
        start = pl.multiple_of(((here + SEQ - shift) & 7) * FRAMES, FRAMES)
        packed_ref[pl.ds(start, FRAMES), :] = piece[...]
    for head in range(2):
        unused_q, unused_k, value, weights = head_weights(packed_ref, head)
        context_ref[:, head * HEAD : (head + 1) * HEAD] = dot(weights.astype(BF), value).astype(BF)


def backward_kernel(packed_ref, own_ref, near_ref, out_ref, grad_s):
    core = lax.axis_index("core")
    for x in range(4):
        for side, ref in ((core, own_ref), (1 - core, near_ref)):
            start = pl.multiple_of((2 * x + side) * FRAMES, FRAMES)
            carried = ref[x * FRAMES : (x + 1) * FRAMES, :].astype(F32)
            text = packed_ref[pl.ds(start, FRAMES), 3 * COLS :].astype(F32)
            grad_s[pl.ds(start, FRAMES), :] = (text + carried).astype(BF)
    for head in range(2):
        base = head * HEAD
        query, key, value, weights = head_weights(packed_ref, head)
        grad = grad_s[:, base : base + HEAD]
        weight_grad = dot_nt(grad, value).astype(BF).astype(F32)
        inner = jnp.sum(weight_grad * weights, axis=1, keepdims=True)
        score_grad = (weights * (weight_grad - inner) * HEAD ** (-0.5)).astype(BF)
        out_ref[:, base : base + HEAD] = dot(score_grad, key).astype(BF)
        out_ref[:, COLS + base : COLS + base + HEAD] = dot_tn(score_grad, query).astype(BF)
        out_ref[:, 2 * COLS + base : 2 * COLS + base + HEAD] = dot_tn(
            weights.astype(BF), grad
        ).astype(BF)


def routing(target_ref, active_ref):
    down = iota((FRAMES, FRAMES), 0)
    across = iota((FRAMES, FRAMES), 1)
    target_row = target_ref[...].astype(F32)
    live_row = (active_ref[...] == 1).astype(F32)
    target_col = jnp.sum(jnp.where(down == across, target_row, 0.0), axis=1, keepdims=True)
    live_col = jnp.sum(jnp.where(down == across, live_row, 0.0), axis=1, keepdims=True)
    same = target_col == target_row
    earlier_row = jnp.sum(jnp.where(same & (down < across), live_col, 0.0), axis=0, keepdims=True)
    earlier_col = jnp.sum(jnp.where(same & (across < down), live_row, 0.0), axis=1, keepdims=True)
    return (target_row, live_row, earlier_row), (target_col, live_col, earlier_col)


def narrow_to_wide(narrow_ref, scratch):
    scratch[...] = narrow_ref[...].astype(F32)
    return jnp.concatenate([scratch[pl.ds(c, SLOTS, stride=8), :] for c in range(8)], axis=1)


def wide_to_narrow(wide, narrow_ref, scratch):
    for c in range(8):
        scratch[pl.ds(c, SLOTS, stride=8), :] = wide[:, c * 128 : (c + 1) * 128]
    narrow_ref[...] = scratch[...].astype(BF)


def send_kernel(parts_ref, target_ref, active_ref, out_ref, narrow_s):
    rows = parts_ref[0].astype(F32)
    for part in range(1, SEQ):
        rows = rows + parts_ref[part].astype(F32)
    (target, live, earlier), unused = routing(target_ref, active_ref)
    slot = iota((SLOTS, FRAMES), 0)
    chosen = (
        (target == (slot >> 1).astype(F32)) & (live > 0.5) & (earlier == (slot & 1).astype(F32))
    ).astype(F32)
    sent = dot(chosen.astype(BF), rows.astype(BF))
    filled = jnp.sum(chosen, axis=1, keepdims=True) > 0.5
    wide_to_narrow(jnp.where(filled, sent, EMPTY), out_ref, narrow_s)


def parts_held():
    x, core = lax.axis_index("x"), lax.axis_index("core")
    return [((x + 4 - shift) & 3) * 2 + side for side in (core, 1 - core) for shift in SHIFTS]


def return_kernel(returned_ref, target_ref, active_ref, out_ref, narrow_s):
    unused, (target, live, earlier) = routing(target_ref, active_ref)
    slot = iota((FRAMES, SLOTS), 1)
    chosen = (
        (target == (slot >> 1).astype(F32)) & (live > 0.5) & (earlier == (slot & 1).astype(F32))
    ).astype(F32)
    returned = narrow_to_wide(returned_ref, narrow_s).astype(BF)
    rows = dot(chosen.astype(BF), returned).astype(BF)
    for x in range(4):
        out_ref[x] = rows


def carry_kernel(rows_ref, own_in_ref, near_in_ref, own_ref, near_ref):
    own_ref[...] = dot_nt(rows_ref[...], own_in_ref[...]).astype(BF)
    near_ref[...] = dot_nt(rows_ref[...], near_in_ref[...]).astype(BF)


def depth_kernel(slots_ref, codes_ref, cot_ref, gain_ref, *refs):
    pieces, refs = refs[:SEQ], refs[SEQ:]
    (
        out_ref,
        weights_s,
        hidden_s,
        cot_s,
        mixed_s,
        projected_s,
        grads_s,
        narrow_s,
        sems,
    ) = refs
    copies = []
    for part, piece in zip(parts_held(), pieces):
        goal = weights_s.at[pl.ds(pl.multiple_of(part * 128, 128), 128), :]
        copies.append(pltpu.make_async_copy(piece, goal, sems.at[len(copies)]))
    for copy in copies:
        copy.start()

    slots = narrow_to_wide(slots_ref, narrow_s).astype(BF)
    live_col = (slots[:, 0:1].astype(F32) < EMPTY * 0.5).astype(F32)
    down = iota((SLOTS, SLOTS), 0)
    across = iota((SLOTS, SLOTS), 1)
    live_row = jnp.sum(jnp.where(down == across, live_col, 0.0), axis=0, keepdims=True)
    rank_row = jnp.sum(jnp.where(down < across, live_col, 0.0), axis=0, keepdims=True)
    rank_col = jnp.sum(jnp.where(across < down, live_row, 0.0), axis=1, keepdims=True)

    spread = (
        (live_row > 0.5) & (rank_row == (iota((PADDED, SLOTS), 0) >> 3).astype(F32))
    ).astype(F32)
    spare = jnp.zeros((PADDED - ROWS, D_DEP), F32)
    hidden = dot(spread.astype(BF), slots) + jnp.concatenate(
        [codes_ref[...].astype(F32), spare], axis=0
    )
    hidden_s[...] = hidden
    cot_s[...] = jnp.concatenate([cot_ref[...].astype(F32), spare], axis=0)
    gain = jnp.concatenate([gain_ref[c : c + 1, :].astype(F32) for c in range(8)], axis=1)
    scale = lax.rsqrt(jnp.sum(hidden * hidden, axis=1, keepdims=True) * (1.0 / D_DEP) + 1e-05)
    normed = (hidden * scale * gain).astype(BF)
    for copy in copies:
        copy.wait()
    width = DHEADS * DHEAD
    w_out = weights_s[:, 3 * width :].reshape(SEQ, 2, DHEAD, width)
    mixed_grad = dot_nt(cot_s[:, :width].astype(BF), w_out[:, 0].reshape(width, width))
    mixed_grad += dot_nt(cot_s[:, width:].astype(BF), w_out[:, 1].reshape(width, width))
    mixed_s[...] = mixed_grad.astype(BF)
    projected_s[...] = dot(normed, weights_s[:, : 3 * width]).astype(BF)

    first_half = iota((GROUP, 128), 1) < DHEAD
    nothing = jnp.zeros((GROUP, 128), BF)
    frame = iota((GROUP // CODES, CODES, 2 * GROUP), 0)
    row = iota((GROUP // CODES, CODES, 2 * GROUP), 2) & (GROUP - 1)
    same_frame = frame == (row >> 3)

    def halves(array):
        return jnp.concatenate(
            [jnp.where(first_half, array, nothing), jnp.where(first_half, nothing, array)], axis=0
        )

    def own_frame(array):
        blocks = array.reshape(GROUP // CODES, CODES, 2 * GROUP)
        return jnp.sum(jnp.where(same_frame, blocks, 0.0), axis=0)

    def all_frames(array):
        blocks = jnp.where(same_frame, array[None], 0.0)
        return blocks.reshape(GROUP, 2 * GROUP).astype(BF)

    units = [
        (slice(group * GROUP, (group + 1) * GROUP), pair * 128)
        for group in range(PADDED // GROUP)
        for pair in range(DHEADS // 2)
    ]
    scores, weight_grad = [], []
    for rows, lanes in units:
        key = projected_s[rows, width + lanes : width + lanes + 128]
        value = projected_s[rows, 2 * width + lanes : 2 * width + lanes + 128]
        scores.append(own_frame(dot_nt(key, halves(projected_s[rows, lanes : lanes + 128]))))
        weight_grad.append(own_frame(dot_nt(value, halves(mixed_s[rows, lanes : lanes + 128]))))
    scores = jnp.concatenate(scores, axis=1) * DHEAD ** (-0.5)
    scores = jnp.where((iota(scores.shape, 0) <= (iota(scores.shape, 1) & 7)), scores, -1e30)
    raised = jnp.exp(scores - jnp.max(scores, axis=0, keepdims=True))
    weights = raised * (1.0 / jnp.sum(raised, axis=0, keepdims=True))
    weight_grad = jnp.concatenate(weight_grad, axis=1).astype(BF).astype(F32)
    inner = jnp.sum(weight_grad * weights, axis=0, keepdims=True)
    score_grad = weights * (weight_grad - inner) * DHEAD ** (-0.5)
    for place, (rows, lanes) in enumerate(units):
        own = slice(place * 2 * GROUP, (place + 1) * 2 * GROUP)
        back = all_frames(score_grad[:, own])
        query_grad = dot_tn(back, projected_s[rows, width + lanes : width + lanes + 128])
        grads_s[rows, lanes : lanes + 128] = jnp.where(
            first_half, query_grad[:GROUP], query_grad[GROUP:]
        ).astype(BF)
        grads_s[rows, width + lanes : width + lanes + 128] = dot(
            back, halves(projected_s[rows, lanes : lanes + 128])
        ).astype(BF)
        grads_s[rows, 2 * width + lanes : 2 * width + lanes + 128] = dot(
            all_frames(weights[:, own]), halves(mixed_s[rows, lanes : lanes + 128])
        ).astype(BF)
    normed_grad = dot_nt(grads_s[...], weights_s[:, : 3 * width]).astype(BF).astype(F32) * gain
    hidden = hidden_s[...]
    inner = jnp.sum(normed_grad * hidden, axis=1, keepdims=True) * (1.0 / D_DEP)
    hidden_grad = cot_s[...] + scale * normed_grad - hidden * (scale * scale * scale * inner)
    frames = jnp.sum(hidden_grad.reshape(FRAMES, CODES, D_DEP), axis=1)

    back = ((live_col > 0.5) & (rank_col == iota((SLOTS, FRAMES), 1).astype(F32))).astype(F32)
    wide_to_narrow(dot(back.astype(BF), frames.astype(BF)), out_ref, narrow_s)


def depth_scratch():
    width = DHEADS * DHEAD
    return [
        pltpu.VMEM((D_DEP, 4 * width), BF),
        pltpu.VMEM((PADDED, D_DEP), F32),
        pltpu.VMEM((PADDED, D_DEP), F32),
        pltpu.VMEM((PADDED, width), BF),
        pltpu.VMEM((PADDED, 3 * width), BF),
        pltpu.VMEM((PADDED, 3 * width), BF),
        pltpu.VMEM((SLOTS * 8, 128), F32),
        pltpu.SemaphoreType.DMA((SEQ,)),
    ]


def exchange(array, axis):
    return lax.all_to_all(array, axis, split_axis=0, concat_axis=0, tiled=True)


def moved(array, axis, size, shift):
    return lax.ppermute(array, axis, [(i, (i + shift) % size) for i in range(size)])


def shards(
    queries,
    keys,
    values,
    text_grad,
    active,
    target,
    codes,
    depth_cot,
    w_in,
    norm_gain,
    w_qkv,
    w_out,
):
    seq = ("x", "core")
    owner = ("y", "z")
    mine = jnp.concatenate([w_in, w_qkv, w_out]).reshape(1, 8, D_DEP)
    along_z = exchange(jnp.broadcast_to(mine, (16, 8, D_DEP)), "z").reshape(128, D_DEP)
    along_y = [along_z] + [moved(along_z, "y", 4, shift) for shift in SHIFTS[1:]]
    block = jax.ShapeDtypeStruct((FRAMES, 4 * COLS), BF)
    blocks = call(pack_kernel, [block] * SEQ, "pack_heads")(
        queries[0], keys[0], values[0], text_grad[0]
    )
    blocks = [blocks[0]] + [moved(blocks[k], seq, SEQ, k) for k in range(1, SEQ)]
    packed, context = call(
        forward_kernel,
        (
            jax.ShapeDtypeStruct((LENGTH, 4 * COLS), BF),
            jax.ShapeDtypeStruct((LENGTH, COLS), BF),
        ),
        "attention_forward",
    )(*blocks)
    own_in, own_rest, parts = call(
        enter_kernel,
        (
            jax.ShapeDtypeStruct((COLS, D_DEP), BF),
            jax.ShapeDtypeStruct((128, 2 * D_DEP), BF),
            jax.ShapeDtypeStruct((LENGTH, D_DEP), BF),
        ),
        "enter_depth",
        scratch_shapes=[pltpu.VMEM((512, D_DEP), BF)],
    )(*along_y, context)
    far_rest = [moved(own_rest, "x", 4, shift) for shift in SHIFTS[1:]]
    parts = exchange(parts.reshape(SEQ, FRAMES, D_DEP), seq)
    parts, near_rest = lax.optimization_barrier((parts, moved(own_rest, "core", 2, 1)))
    rest = [own_rest, *far_rest, near_rest] + [moved(piece, "core", 2, 1) for piece in far_rest]
    narrow = jax.ShapeDtypeStruct((SLOTS * 8, 128), BF)
    sent = call(
        send_kernel, narrow, "send_rows", scratch_shapes=[pltpu.VMEM((SLOTS * 8, 128), F32)]
    )(parts, target, active)
    slots = exchange(sent.reshape(OWNERS, 16, 128), owner).reshape(SLOTS * 8, 128)
    vmem = pl.BlockSpec(memory_space=pltpu.VMEM)
    anywhere = pl.BlockSpec(memory_space=pl.ANY)
    grads = call(
        depth_kernel,
        narrow,
        "depth_layer",
        in_specs=[vmem] * 4 + [anywhere] * SEQ,
        out_specs=vmem,
        scratch_shapes=depth_scratch(),
        vmem=58,
    )(
        slots,
        codes.reshape(ROWS, D_DEP),
        depth_cot.reshape(ROWS, D_DEP),
        norm_gain.reshape(8, 128),
        *rest,
    )
    late_in, unused = lax.optimization_barrier((own_in, grads))
    near_in = moved(late_in, "core", 2, 1)
    returned = exchange(grads.reshape(OWNERS, 16, 128), owner).reshape(SLOTS * 8, 128)
    rows = call(
        return_kernel,
        jax.ShapeDtypeStruct((4, FRAMES, D_DEP), BF),
        "return_rows",
        scratch_shapes=[pltpu.VMEM((SLOTS * 8, 128), F32)],
    )(returned, target, active)
    rows = exchange(rows, "x").reshape(4 * FRAMES, D_DEP)
    half = jax.ShapeDtypeStruct((4 * FRAMES, COLS), BF)
    own_carried, near_carried = call(carry_kernel, (half, half), "context_grads")(
        rows, own_in, near_in
    )
    grads = call(
        backward_kernel,
        jax.ShapeDtypeStruct((LENGTH, 3 * COLS), BF),
        "attention_backward",
        scratch_shapes=[pltpu.VMEM((LENGTH, COLS), BF)],
    )(packed, own_carried, moved(near_carried, "core", 2, 1))
    grads = exchange(grads.reshape(SEQ, FRAMES, 3 * COLS), seq)
    shape = jax.ShapeDtypeStruct((FRAMES, D_CTX), BF)
    query_grad, key_grad, value_grad = call(unpack_kernel, (shape, shape, shape), "unpack_grads")(grads)
    return query_grad[None], key_grad[None], value_grad[None]


def solution(mesh):
    split = Mesh(mesh.devices.reshape(4, 2, 4, 16), ("x", "core", "y", "z"))
    rows = P(("y", "z"), ("x", "core"), None)
    frames = P(("y", "z"), ("x", "core"))
    code_rows = P(("y", "z"), ("x", "core"), None, None)
    flat = P(("x", "core", "y", "z"))
    in_specs = (
        rows,
        rows,
        rows,
        rows,
        frames,
        frames,
        code_rows,
        code_rows,
        flat,
        P(),
        flat,
        flat,
    )
    return jax.shard_map(
        shards, mesh=split, in_specs=in_specs, out_specs=(rows, rows, rows), check_vma=False
    )
```
